128 devices in a mesh: lat: 8 (over y_lo, x), lon: 16 (over y_hi, z, core).
Axes of the slice: x: 4, y: 4 (y_hi: 2, y_lo: 2; y = y_hi * 2 + y_lo), z: 4, core: 2. Of those that a mesh axis runs over, the one named last changes fastest.
Arguments:
- tokens: bfloat16 [4, 4, 48, 192, 512], P(None, None, 'lat', 'lon'), may hold values from -6 to 6
- norm1_gain: float32 [512], replicated, may hold values from 0.1 to 1.9
- qkv1: bfloat16 [512, 1536], replicated, may hold values from -1.5 to 1.5, as said below
- proj1: bfloat16 [512, 512], replicated, may hold values from -0.25 to 0.25
- norm2_gain: float32 [512], replicated, may hold values from 0.1 to 1.9
- mlp_in: bfloat16 [512, 2048], replicated, may hold values from -0.25 to 0.25
- mlp_out: bfloat16 [2048, 512], replicated, may hold values from -0.125 to 0.125
- merge_gain: float32 [2048], replicated, may hold values from 0.1 to 1.9
- merge_weight: bfloat16 [2048, 1024], replicated, may hold values from -0.125 to 0.125
- norm3_gain: float32 [1024], replicated, may hold values from 0.1 to 1.9
- qkv2: bfloat16 [1024, 3072], replicated, may hold values from -1.5 to 1.5, as said below
- proj2: bfloat16 [1024, 1024], replicated, may hold values from -0.1875 to 0.1875
Outputs:
- level1_out: bfloat16 [4, 4, 48, 192, 512], P(None, None, 'lat', 'lon')
- level2_out: bfloat16 [4, 4, 24, 96, 1024], P(None, None, 'lat')
The draws below stay inside these ranges and needn't reach their ends.
Inputs may be any that keep to these rules, and one draw needn't show every extreme that they name: `qkv1`: columns hold the query, key and value projections in that order, heads contiguous. `qkv2`: columns hold the query, key and value projections in that order, heads contiguous.
All inputs are finite; a program needn't handle non-finite values.
Results may differ from the reference program's by a relative error of at most 0.015.
Values may be sent and summed in bfloat16 or wider, within the bound.
A program may use at most 256 MiB of HBM per device.

```python
import jax
import jax.numpy as jnp
from jax import lax

D = 512
HEADS1 = 8
HEADS2 = 16
MEMBERS = 4
LEVELS = 4
WIN_LEV = 2
WIN_LAT = 6
WIN_LON = 12
NLAT = 48
NLON = 192


def projection(key, rows, heads, align):
    first, second = jax.random.split(key, 2)
    drawn = jax.random.normal(first, (rows, 3 * rows), jnp.float32) * rows ** (-0.5)
    strength = 1.0 + 5.0 * jax.random.uniform(second, (heads,), jnp.float32)
    column_strength = jnp.repeat(strength, rows // heads)
    query = drawn[:, :rows] * (1.0 + align * (column_strength - 1.0))
    keyed = drawn[:, rows:2 * rows]
    joined = jnp.concatenate([query, keyed, drawn[:, 2 * rows:]], axis=1)
    return jnp.clip(joined, -1.5, 1.5).astype(jnp.bfloat16)


def draw_qkv1(key, part):
    key = jax.random.fold_in(key, 11)
    return projection(key, D, HEADS1, 0.0)


def draw_qkv2(key, part):
    key = jax.random.fold_in(key, 12)
    return projection(key, 2 * D, HEADS2, 0.0)


def block_levels(rng, shape, cuts, smallest, high):
    def one(dim, blocks):
        draws = jax.random.uniform(jax.random.fold_in(jax.random.fold_in(rng, 6), dim), (blocks,), jnp.float32, smallest / len(cuts), high / len(cuts))
        return jnp.repeat(jnp.exp(draws), shape[dim] // blocks).reshape((-1,) + (1,) * (len(shape) - dim - 1))

    loudness = one(*cuts[0])
    for cut in cuts[1:]:
        loudness = loudness * one(*cut)
    return loudness


def scatter_about(stream_key, extent, deviation, bound, cuts=(), dtype=jnp.bfloat16):
    values = deviation * jax.random.normal(stream_key, extent, jnp.float32)
    if cuts:
        values = values * block_levels(stream_key, extent, cuts, -0.22, 0.18)
    return jnp.clip(values, -bound, bound).astype(dtype)


def setup_inputs(seed: int = 0) -> dict:
    streams_of = jax.random.split(jax.random.key(seed), 13)
    return {
        "tokens": scatter_about(streams_of[0], (MEMBERS, LEVELS, NLAT, NLON, D), 1.0, 6.0, ((2, 8), (3, 16))),
        "norm1_gain": jnp.clip(1.0 + 0.18 * jax.random.normal(streams_of[1], (D,), jnp.float32), 0.1, 1.9),
        "qkv1": draw_qkv1(jax.random.fold_in(streams_of[12], 71), 0),
        "proj1": scatter_about(streams_of[3], (D, D), D ** -0.5, 0.25),
        "norm2_gain": jnp.clip(1.0 + 0.18 * jax.random.normal(streams_of[4], (D,), jnp.float32), 0.1, 1.9),
        "mlp_in": scatter_about(streams_of[5], (D, 4 * D), D ** -0.5, 0.25),
        "mlp_out": scatter_about(streams_of[6], (4 * D, D), (4 * D) ** -0.5, 0.125),
        "merge_gain": jnp.clip(1.0 + 0.18 * jax.random.normal(streams_of[7], (4 * D,), jnp.float32), 0.1, 1.9),
        "merge_weight": scatter_about(streams_of[8], (4 * D, 2 * D), (4 * D) ** -0.5, 0.125),
        "norm3_gain": jnp.clip(1.0 + 0.18 * jax.random.normal(streams_of[9], (2 * D,), jnp.float32), 0.1, 1.9),
        "qkv2": draw_qkv2(jax.random.fold_in(streams_of[12], 71), 0),
        "proj2": scatter_about(streams_of[11], (2 * D, 2 * D), (2 * D) ** -0.5, 0.1875),
    }


def layer_norm(values, gain):
    mean = lax.optimization_barrier(jnp.mean(values, -1, keepdims=True))
    centred = values - mean
    spread = lax.optimization_barrier(jnp.mean(centred * centred, -1, keepdims=True))
    return centred * lax.rsqrt(spread + 1e-05) * gain

def window_attend(queries, keys, values, allow, heads):
    count, qlen, width = queries.shape
    klen = keys.shape[1]
    size = width // heads
    q_four = queries.astype(jnp.float32).reshape(count, qlen, heads, size)
    k_four = keys.astype(jnp.float32).reshape(count, klen, heads, size)
    v_four = values.astype(jnp.float32).reshape(count, klen, heads, size)
    scores = jnp.einsum('wqhd,wkhd->whqk', q_four, k_four) * size ** (-0.5)
    if allow is not None:
        scores = jnp.where(allow[:, None], scores, -1e+30)
    top = lax.optimization_barrier(jnp.max(scores, -1, keepdims=True))
    weights = jnp.exp(scores - top)
    probs = (weights / lax.optimization_barrier(jnp.sum(weights, -1, keepdims=True))).astype(jnp.bfloat16)
    mixed = jnp.einsum('whqk,wkhd->wqhd', probs.astype(jnp.float32), v_four)
    return mixed.astype(jnp.bfloat16).reshape(count, qlen, width)

def reference(tokens, norm1_gain, qkv1, proj1, norm2_gain, mlp_in, mlp_out, merge_gain, merge_weight, norm3_gain, qkv2, proj2):
    members = tokens.shape[0]
    half_lat = WIN_LAT // 2
    half_lon = WIN_LON // 2
    half_lev = WIN_LEV // 2
    cells = WIN_LEV * WIN_LAT * WIN_LON
    inputs = tokens.astype(jnp.float32)
    normed = layer_norm(inputs, norm1_gain).astype(jnp.bfloat16)
    project = jnp.dot(normed.reshape(-1, D), qkv1, preferred_element_type=jnp.float32).astype(jnp.bfloat16)
    project = project.reshape(members, LEVELS, NLAT, NLON, 3 * D)
    lat_windows = (NLAT + WIN_LAT) // WIN_LAT
    lon_windows = NLON // WIN_LON
    lev_windows = (LEVELS + WIN_LEV) // WIN_LEV
    rows_seen = jnp.arange(NLAT + WIN_LAT)
    keep_rows = (rows_seen >= half_lat) & (rows_seen < NLAT + half_lat)
    levels_seen = jnp.arange(LEVELS + WIN_LEV)
    keep_levels = (levels_seen >= half_lev) & (levels_seen < LEVELS + half_lev)
    keep = keep_levels.reshape(lev_windows, 1, 1, WIN_LEV, 1, 1) & keep_rows.reshape(1, lat_windows, 1, 1, WIN_LAT, 1)
    keep = jnp.broadcast_to(keep, (lev_windows, lat_windows, lon_windows, WIN_LEV, WIN_LAT, WIN_LON))
    keep = keep.reshape(lev_windows * lat_windows, lon_windows, cells)

    def attend_first(item):
        block, mask = item
        return window_attend(block[..., :D], block[..., D:2 * D], block[..., 2 * D:], mask[:, None, :], HEADS1)

    def first_level(block):
        padded = jnp.pad(block, ((half_lev, half_lev), (half_lat, half_lat), (0, 0), (0, 0)))
        padded = jnp.roll(padded, half_lon, axis=2)
        grouped = padded.reshape(lev_windows, WIN_LEV, lat_windows, WIN_LAT, lon_windows, WIN_LON, 3 * D)
        grouped = grouped.transpose(0, 2, 4, 1, 3, 5, 6).reshape(lev_windows * lat_windows, lon_windows, cells, 3 * D)
        attended = lax.map(attend_first, (grouped, keep))
        attended = attended.reshape(lev_windows, lat_windows, lon_windows, WIN_LEV, WIN_LAT, WIN_LON, D)
        attended = attended.transpose(0, 3, 1, 4, 2, 5, 6).reshape(LEVELS + WIN_LEV, NLAT + WIN_LAT, NLON, D)
        return jnp.roll(attended[half_lev:half_lev + LEVELS, half_lat:half_lat + NLAT], -half_lon, axis=2)
    attended = lax.map(first_level, project).reshape(-1, D)
    mid = inputs.reshape(-1, D) + jnp.dot(attended, proj1, preferred_element_type=jnp.float32)
    normed_two = layer_norm(mid, norm2_gain).astype(jnp.bfloat16)
    hidden = jax.nn.gelu(jnp.dot(normed_two, mlp_in, preferred_element_type=jnp.float32), approximate=False).astype(jnp.bfloat16)
    level_one = (mid + jnp.dot(hidden, mlp_out, preferred_element_type=jnp.float32)).astype(jnp.bfloat16)
    coarse_lat = NLAT // 2
    coarse_lon = NLON // 2
    stacked = level_one.astype(jnp.float32).reshape(members, LEVELS, coarse_lat, 2, coarse_lon, 2, D)
    stacked = stacked.transpose(0, 1, 2, 4, 3, 5, 6).reshape(-1, 4 * D)
    merged = layer_norm(stacked, merge_gain).astype(jnp.bfloat16)
    coarse = jnp.dot(merged, merge_weight, preferred_element_type=jnp.float32).astype(jnp.bfloat16)
    normed_three = layer_norm(coarse.astype(jnp.float32), norm3_gain).astype(jnp.bfloat16)
    project_two = jnp.dot(normed_three, qkv2, preferred_element_type=jnp.float32).astype(jnp.bfloat16)
    rows_two = coarse_lat // WIN_LAT
    cols_two = coarse_lon // WIN_LON
    lev_two = LEVELS // WIN_LEV
    project_two = project_two.reshape(members, lev_two, WIN_LEV, rows_two, WIN_LAT, cols_two, WIN_LON, 6 * D)
    project_two = project_two.transpose(0, 1, 3, 5, 2, 4, 6, 7).reshape(members * lev_two * rows_two, cols_two, cells, 6 * D)

    def attend_second(block):
        return window_attend(block[..., :2 * D], block[..., 2 * D:4 * D], block[..., 4 * D:], None, HEADS2)
    attended_two = lax.map(attend_second, project_two)
    attended_two = attended_two.reshape(members, lev_two, rows_two, cols_two, WIN_LEV, WIN_LAT, WIN_LON, 2 * D)
    attended_two = attended_two.transpose(0, 1, 4, 2, 5, 3, 6, 7).reshape(-1, 2 * D)
    level_two = coarse.astype(jnp.float32) + jnp.dot(attended_two, proj2, preferred_element_type=jnp.float32)
    level_one = level_one.reshape(members, LEVELS, NLAT, NLON, D)
    level_two = level_two.astype(jnp.bfloat16).reshape(members, LEVELS, coarse_lat, coarse_lon, 2 * D)
    return (level_one, level_two)
```

```python
import functools

import jax
import jax.numpy as jnp
import ml_dtypes
import numpy as np
from jax import lax
from jax.experimental import pallas as pl
from jax.experimental.pallas import tpu as pltpu
from jax.sharding import PartitionSpec as P

F32 = jnp.float32
BF16 = jnp.bfloat16
MESH = pl.DeviceIdType.MESH

MEMBERS, LEVELS, ROWS, COLS, D = 4, 4, 6, 12, 512
CELLS = LEVELS * ROWS * COLS
QUAD = CELLS // 4
PAD = 16
PADDED = LEVELS * ROWS * PAD
LAT, LON = 8, 16
CROWS, CCOLS, D2 = 3, 6, 1024
HEADS2 = 16
HALF = 144


def quad_cells():
    cells = []
    for rh in range(2):
        for ch in range(2):
            for levels in ((1, 2), (0, 3)):
                for lev in levels:
                    for r in range(3):
                        for c in range(6):
                            cells.append((lev, rh * 3 + r, ch * 6 + c))
    return cells


def one_hot(rows, width):
    out = np.zeros((len(rows), width), ml_dtypes.bfloat16)
    out[np.arange(len(rows)), rows] = 1
    return out


def reorderings():
    cells = quad_cells()
    place = {cell: i for i, cell in enumerate(cells)}
    gather = one_hot([(lev * ROWS + r) * PAD + c for lev, r, c in cells], PADDED)
    scatter = np.ascontiguousarray(gather.T)
    window_rows = [q * 72 + lp * 36 + i for lp in range(2) for q in range(4) for i in range(36)]
    to_window = one_hot(window_rows, CELLS)
    from_window = np.ascontiguousarray(to_window.T)
    merge = one_hot(
        [
            place[(lev, 2 * a + da, 2 * b + db)]
            for da in range(2)
            for db in range(2)
            for lev in range(LEVELS)
            for a in range(CROWS)
            for b in range(CCOLS)
        ],
        CELLS,
    )
    band = one_hot(
        [d * 72 + k * 6 + c for k in range(12) for d in range(4) for c in range(6)], CELLS
    )
    return gather, scatter, to_window, from_window, merge, band


def dot(a, b):
    return jnp.dot(a, b, preferred_element_type=F32)


def dot_t(a, b):
    return lax.dot_general(a, b, (((1,), (1,)), ((), ())), preferred_element_type=F32)


def norm_rows(values):
    mean = jnp.mean(values, -1, keepdims=True)
    centred = values - mean
    spread = jnp.mean(centred * centred, -1, keepdims=True)
    return centred * lax.rsqrt(spread + 1e-05)


def gelu(v):
    return 0.5 * v * (1.0 + lax.erf(v * np.float32(2.0**-0.5)))


def stack_slabs(ref, m):
    return jnp.concatenate([ref[m, q].astype(F32) for q in range(4)], axis=0).astype(BF16)


def attend(q_ref, q_rows, k_rows, q_at, k_at, v_at, bias):
    rows = q_rows[1]
    qp = q_ref[pl.ds(*q_rows), q_at : q_at + 128]
    kp = q_ref[pl.ds(*k_rows), k_at : k_at + 128]
    vp = q_ref[pl.ds(*k_rows), v_at : v_at + 128]
    first = lax.broadcasted_iota(jnp.int32, (rows, 128), 1) < 64
    outs = []
    for head in range(2):
        keep = first if head == 0 else ~first
        qh = jnp.where(keep, qp, jnp.zeros_like(qp))
        scores = dot_t(qh, kp) * 0.125 + bias
        weights = jnp.exp(scores - jnp.max(scores, -1, keepdims=True))
        total = jnp.sum(weights, -1, keepdims=True)
        outs.append(dot(weights.astype(BF16), vp) / total)
    return jnp.where(first, outs[0], outs[1])


def body(
    tok, gain1, gain2, gain_m, gain3, gather, scatter, to_win, from_win, merge, band,
    qkv1_h, proj1_h, in_h, out_h, mw_h, qkv2_h, proj2_h,
    l1, l2,
    qkv1, proj1, w_in, w_out, mw, qkv2, proj2,
    pad, xs, nrm, win, qkv, att, bko, bki, mid, acc, coarse, nc, qkv_b, o2, at2, g, stage,
    bias1, bias2,
    w_sem, hs, hr, bs, br, cs, cr, as_, ar, gs, gr, st_sem,
):
    lat, lon = lax.axis_index("lat"), lax.axis_index("lon")
    north, south = lax.rem(lat + LAT - 1, LAT), lax.rem(lat + 1, LAT)
    west, east = lax.rem(lon + LON - 1, LON), lax.rem(lon + 1, LON)
    core = lax.rem(lon, 2)
    z = lax.rem(lon // 2, 4)
    yh = lon // 8
    lon_y = lax.rem(lon + 8, LON)
    zp, zm = lax.rem(z + 1, 4), lax.rem(z + 3, 4)
    z_far = lax.rem(z + 2, 4)
    other = lon + 1 - 2 * core

    def at(y, zz):
        return y * 8 + zz * 2 + core

    lon_zp, lon_zm = at(yh, zp), at(yh, zm)
    group_lat, group_lon = lat - lax.rem(lat, 2), lon - core
    mine = 2 * lax.rem(lat, 2) + core
    peers = []
    for k in range(1, 4):
        j = lax.rem(mine + k, 4)
        peers.append((j, (group_lat + j // 2, group_lon + lax.rem(j, 2))))

    to_nbr = [(north, west), (north, lon), (lat, west)]
    from_nbr = [(south, east), (south, lon), (lat, east)]

    loads = []
    wide = HEADS2 // 4 * 64
    for i, (src, dst) in enumerate(
        [(qkv1_h, qkv1), (proj1_h, proj1), (in_h, w_in), (out_h, w_out), (mw_h, mw)]
    ):
        loads.append(pltpu.make_async_copy(src, dst, w_sem.at[i]))
    for part in range(3):
        columns = pl.ds(pl.multiple_of(part * D2 + mine * wide, wide), wide)
        loads.append(
            pltpu.make_async_copy(
                qkv2_h.at[:, columns], qkv2.at[:, pl.ds(part * wide, wide)], w_sem.at[5 + part]
            )
        )
    loads.append(pltpu.make_async_copy(proj2_h, proj2, w_sem.at[8]))
    for load in loads:
        load.start()

    barrier = pltpu.get_barrier_semaphore()
    partners = to_nbr + from_nbr + [dev for _, dev in peers]
    partners += [(lat, lon_y), (lat, lon_zp), (lat, lon_zm)]
    for dev in partners:
        pl.semaphore_signal(barrier, inc=1, device_id=dev, device_id_type=MESH)

    def remote(src, dst, send, recv, dev):
        return pltpu.make_async_remote_copy(
            src_ref=src, dst_ref=dst, send_sem=send, recv_sem=recv, device_id=dev, device_id_type=MESH
        )

    def halo(m, q):
        return remote(nrm.at[m, q], win.at[m, q], hs.at[m, q], hr.at[m, q], to_nbr[q])

    def back(m, q):
        return remote(bko.at[m, q], bki.at[m, q], bs.at[m, q], br.at[m, q], from_nbr[q])

    def spread(m, k):
        j, dev = peers[k]
        return remote(nc.at[m, mine], nc.at[m, mine], cs.at[m, k], cr.at[m, mine], dev)

    def spread_arrival(m, k):
        j, dev = peers[k]
        return remote(nc.at[m, j], nc.at[m, j], cs.at[m, k], cr.at[m, j], dev)

    def result(m, k):
        j, dev = peers[k]
        return remote(o2.at[m, j], at2.at[m, mine], as_.at[m, k], ar.at[m, mine], dev)

    def result_arrival(m, k):
        j, dev = peers[k]
        return remote(o2.at[m, j], at2.at[m, j], as_.at[m, k], ar.at[m, j], dev)

    def block(m, slot, send, dev):
        return remote(g.at[m, slot], g.at[m, slot], gs.at[m, send], gr.at[m, slot], (lat, dev))

    def arrived(m, slot):
        block(m, slot, 0, lon_y).wait_recv()

    def blocks_of(shape, dim, size):
        return lax.broadcasted_iota(jnp.int32, shape, dim) // size

    shape = (HALF, HALF)
    south_q = blocks_of(shape, 0, 72) != blocks_of(shape, 1, 72)
    level_a = lax.rem(blocks_of(shape, 0, 18), 2) != lax.rem(blocks_of(shape, 1, 18), 2)
    edge = jnp.where(lat == LAT - 1, np.float32(-1e30), np.float32(0.0))
    rows_bias = jnp.where(south_q, edge, 0.0)
    bias1[0] = rows_bias
    bias1[1] = jnp.where(level_a, np.float32(-1e30), rows_bias)
    shape = (CELLS, CELLS)
    level_b = lax.rem(blocks_of(shape, 0, 36), 2) != lax.rem(blocks_of(shape, 1, 36), 2)
    bias2[...] = jnp.where(level_b, np.float32(-1e30), np.float32(0.0))

    pad[...] = jnp.zeros_like(pad)
    pl.semaphore_wait(barrier, len(partners))

    def start_member(m, carry):
        pad[:, 0:COLS, :] = tok[m].reshape(LEVELS * ROWS, COLS, D)
        x = dot(gather[...], pad[...].reshape(PADDED, D))
        xs[m] = x.astype(BF16)
        normed = (norm_rows(x) * gain1[...])
        for q in range(3):
            nrm[m, q] = normed[q * QUAD : (q + 1) * QUAD].astype(BF16)
            halo(m, q).start()
        win[m, 3] = normed[3 * QUAD :].astype(BF16)
        return carry

    lax.fori_loop(0, MEMBERS, start_member, 0)

    def window_attention(m):
        for q in range(3):
            halo(m, q).wait_recv()
        cells = dot(to_win[...], stack_slabs(win, m)).astype(BF16)
        for part in range(3):
            columns = slice(part * D, (part + 1) * D)
            qkv[:, columns] = dot(cells, qkv1[:, columns]).astype(BF16)
        for lp in range(2):
            rows = (lp * HALF, HALF)
            for pair in range(4):
                columns = pair * 128
                att[lp * HALF : (lp + 1) * HALF, columns : columns + 128] = attend(
                    qkv, rows, rows, columns, D + columns, 2 * D + columns, bias1[lp]
                ).astype(BF16)
        tile = dot(from_win[...], att[...])
        for q in range(3):
            bko[m, q] = tile[q * QUAD : (q + 1) * QUAD].astype(BF16)
            back(m, q).start()
        bki[m, 3] = tile[3 * QUAD :].astype(BF16)

    def feed_forward(m):
        for q in range(3):
            back(m, q).wait_recv()
        mid[...] = xs[m].astype(F32) + dot(stack_slabs(bki, m), proj1[...])
        normed = (norm_rows(mid[...]) * gain2[...]).astype(BF16)
        for part in range(4):
            columns = slice(part * D, (part + 1) * D)
            hidden = gelu(dot(normed, w_in[:, columns])).astype(BF16)
            partial = dot(hidden, w_out[columns, :])
            if part == 0:
                acc[...] = mid[...] + partial
            else:
                acc[...] += partial
        level1 = acc[...].astype(BF16)
        spread_out = dot(scatter[...], level1).astype(BF16).reshape(LEVELS * ROWS, PAD, D)
        l1[m] = spread_out[:, 0:COLS, :].reshape(LEVELS, ROWS, COLS, D)
        quarters = dot(merge[...], level1)
        parts = [quarters[k * QUAD : (k + 1) * QUAD] for k in range(4)]
        mean = sum(jnp.sum(p, -1, keepdims=True) for p in parts) * (1.0 / (4 * D))
        parts = [p - mean for p in parts]
        var = sum(jnp.sum(p * p, -1, keepdims=True) for p in parts) * (1.0 / (4 * D))
        scale = lax.rsqrt(var + 1e-05)
        merged = jnp.concatenate(
            [(p * scale * gain_m[:, k * D : (k + 1) * D]).astype(BF16) for k, p in enumerate(parts)],
            axis=1,
        )
        small = dot(merged, mw[...]).astype(BF16)
        coarse[m] = small
        nc[m, mine] = (norm_rows(small.astype(F32)) * gain3[...]).astype(BF16)
        for k in range(3):
            spread(m, k).start()

    def heads_of_group(m):
        for k in range(3):
            spread_arrival(m, k).wait_recv()
        qkv_b[...] = dot(stack_slabs(nc, m), qkv2[...]).astype(BF16)
        rows = (0, CELLS)
        for pair in range(2):
            columns = pair * 128
            out = attend(qkv_b, rows, rows, columns, wide + columns, 2 * wide + columns, bias2[...])
            for d in range(4):
                o2[m, d, :, columns : columns + 128] = out[d * QUAD : (d + 1) * QUAD].astype(BF16)
        for k in range(3):
            result(m, k).start()
        at2[m, mine] = o2[m, mine]

    def project_out(m):
        for k in range(3):
            result_arrival(m, k).wait_recv()
        attended = jnp.concatenate([at2[m, j] for j in range(4)], axis=1)
        level2 = coarse[m].astype(F32) + dot(attended, proj2[...])
        g[m, lon] = level2.astype(BF16)
        block(m, lon, 0, lon_y).start()
        block(m, lon, 1, lon_zp).start()
        block(m, lon, 2, lon_zm).start()
        block(m, lon, 3, other).start()

    def after_y(m):
        arrived(m, lon_y)
        block(m, lon_y, 4, lon_zp).start()
        block(m, lon_y, 5, lon_zm).start()
        block(m, lon_y, 6, other).start()

    toward = 1 - 2 * core
    z_from = lax.rem(z + 4 - toward, 4)
    z_to = lax.rem(z + 4 + toward, 4)

    def after_z(m):
        for y in range(2):
            arrived(m, at(y, z_from))
            block(m, at(y, z_from), 7 + y, at(yh, z_to)).start()
            block(m, at(y, z_from), 9 + y, other).start()
        for y in range(2):
            arrived(m, at(y, z_to))
            block(m, at(y, z_to), 11 + y, other).start()

    def after_z2(m):
        for y in range(2):
            arrived(m, at(y, z_far))
            block(m, at(y, z_far), 13 + y, other).start()

    def put_out(m):
        return pltpu.make_async_copy(stage.at[lax.rem(m, 2)], l2.at[m], st_sem.at[lax.rem(m, 2)])

    def lay_out(m):
        for y in range(2):
            for zz in range(4):
                arrived(m, y * 8 + zz * 2 + 1 - core)

        @pl.when(m >= 2)
        def _():
            put_out(m - 2).wait()

        for half in range(2):
            pieces = []
            for quarter in range(2):
                first = half * 8 + quarter * 4
                slabs = jnp.concatenate([g[m, first + d].astype(F32) for d in range(4)], axis=0)
                pieces.append(dot(band[...], slabs.astype(BF16)).reshape(12, 24, D2))
            columns = jnp.concatenate(pieces, axis=1).astype(BF16)
            stage[lax.rem(m, 2), :, :, half * 48 : (half + 1) * 48, :] = columns.reshape(
                LEVELS, CROWS, 48, D2
            )
        put_out(m).start()

    def when(t, lo, hi, phase, lag):
        @pl.when((t >= lo) & (t < hi))
        def _():
            phase(t - lag)

    def step(t, carry):
        when(t, 3, 7, project_out, 3)
        when(t, 6, 8, after_z, 4)

        @pl.when(t == 2)
        def _():
            for i in range(5, 9):
                loads[i].wait()

        when(t, 2, 6, heads_of_group, 2)
        when(t, 3, 7, after_y, 3)
        when(t, 4, 8, after_z2, 4)

        @pl.when(t == 1)
        def _():
            for i in range(1, 5):
                loads[i].wait()

        when(t, 1, 5, feed_forward, 1)
        when(t, 3, 5, after_z, 3)

        @pl.when(t == 0)
        def _():
            loads[0].wait()

        when(t, 0, 4, window_attention, 0)
        when(t, 5, 9, lay_out, 5)
        return carry

    lax.fori_loop(0, 9, step, 0)

    def finish(m, carry):
        for q in range(3):
            halo(m, q).wait_send()
            back(m, q).wait_send()
            spread(m, q).wait_send()
            result(m, q).wait_send()
        for i in range(15):
            block(m, lon, i, lon_y).wait_send()
        return carry

    lax.fori_loop(0, MEMBERS, finish, 0)
    put_out(MEMBERS - 2).wait()
    put_out(MEMBERS - 1).wait()


def shards(
    tokens, norm1_gain, qkv1, proj1, norm2_gain, mlp_in, mlp_out, merge_gain, merge_weight,
    norm3_gain, qkv2, proj2,
):
    vmem = pl.BlockSpec(memory_space=pltpu.VMEM)
    hbm = pl.BlockSpec(memory_space=pl.ANY)
    dma = pltpu.SemaphoreType.DMA
    wide = HEADS2 // 4 * 64

    def bf(*dims):
        return pltpu.VMEM(dims, BF16)

    def fl(*dims):
        return pltpu.VMEM(dims, F32)

    level1, level2 = pl.pallas_call(
        body,
        name="encoder",
        out_shape=(
            jax.ShapeDtypeStruct((MEMBERS, LEVELS, ROWS, COLS, D), BF16),
            jax.ShapeDtypeStruct((MEMBERS, LEVELS, CROWS, LON * CCOLS, D2), BF16),
        ),
        in_specs=[vmem] * 11 + [hbm] * 7,
        out_specs=(vmem, hbm),
        scratch_shapes=[
            bf(D, 3 * D), bf(D, D), bf(D, 4 * D), bf(4 * D, D), bf(4 * D, D2), bf(D2, 3 * wide),
            bf(D2, D2),
            bf(LEVELS * ROWS, PAD, D),
            bf(MEMBERS, CELLS, D),
            bf(MEMBERS, 3, QUAD, D), bf(MEMBERS, 4, QUAD, D),
            bf(CELLS, 3 * D), bf(CELLS, D),
            bf(MEMBERS, 3, QUAD, D), bf(MEMBERS, 4, QUAD, D),
            fl(CELLS, D), fl(CELLS, D),
            bf(MEMBERS, QUAD, D2), bf(MEMBERS, 4, QUAD, D2),
            bf(CELLS, 3 * wide),
            bf(MEMBERS, 4, QUAD, wide), bf(MEMBERS, 4, QUAD, wide),
            bf(MEMBERS, LON, QUAD, D2),
            bf(2, LEVELS, CROWS, LON * CCOLS, D2),
            fl(2, HALF, HALF), fl(CELLS, CELLS),
            dma((9,)),
            dma((MEMBERS, 3)), dma((MEMBERS, 3)),
            dma((MEMBERS, 3)), dma((MEMBERS, 3)),
            dma((MEMBERS, 3)), dma((MEMBERS, 4)),
            dma((MEMBERS, 3)), dma((MEMBERS, 4)),
            dma((MEMBERS, 15)), dma((MEMBERS, LON)),
            dma((2,)),
        ],
        compiler_params=pltpu.CompilerParams(
            collective_id=0, has_side_effects=True, vmem_limit_bytes=60 * 2**20
        ),
        cost_estimate=pl.CostEstimate(flops=12 * 10**9, bytes_accessed=30 * 10**6, transcendentals=4 * 10**6),
    )(
        tokens, norm1_gain.reshape(1, D), norm2_gain.reshape(1, D), merge_gain.reshape(1, 4 * D),
        norm3_gain.reshape(1, D2), *[jnp.asarray(order) for order in reorderings()],
        qkv1, proj1, mlp_in, mlp_out, merge_weight, qkv2, proj2,
    )
    return level1, level2


def solution(mesh):
    in_specs = (P(None, None, "lat", "lon", None),) + (P(),) * 11
    out_specs = (P(None, None, "lat", "lon", None), P(None, None, "lat", None, None))
    return jax.shard_map(shards, mesh=mesh, in_specs=in_specs, out_specs=out_specs, check_vma=False)
```

```python
import functools

import jax
import jax.numpy as jnp
import ml_dtypes
import numpy as np
from jax import lax
from jax.experimental import pallas as pl
from jax.experimental.pallas import tpu as pltpu
from jax.sharding import PartitionSpec as P

F32 = jnp.float32
BF16 = jnp.bfloat16
MESH = pl.DeviceIdType.MESH

MEMBERS, LEVELS, ROWS, COLS, D = 4, 4, 6, 12, 512
CELLS = LEVELS * ROWS * COLS
QUAD = CELLS // 4
SLAB = 40
LAT, LON = 8, 16
CROWS, CCOLS, D2 = 3, 6, 1024
HEADS2 = 16
HALF = 144


def quad_cells():
    cells = []
    for rh in range(2):
        for ch in range(2):
            for levels in ((1, 2), (0, 3)):
                for lev in levels:
                    for r in range(3):
                        for c in range(6):
                            cells.append((lev, rh * 3 + r, ch * 6 + c))
    return cells


def one_hot(rows, width):
    out = np.zeros((len(rows), width), ml_dtypes.bfloat16)
    for i, row in enumerate(rows):
        if row >= 0:
            out[i, row] = 1
    return out


def reorderings():
    cells = quad_cells()
    place = {cell: i for i, cell in enumerate(cells)}
    gather = one_hot([(r * COLS + c) * LEVELS + lev for lev, r, c in cells], CELLS)
    scatter = np.ascontiguousarray(gather.T)
    window_rows = [q * 72 + lp * 36 + i for lp in range(2) for q in range(4) for i in range(36)]
    to_window = one_hot(window_rows, CELLS)
    from_window = np.ascontiguousarray(to_window.T)
    coarse_cells = [(lev, a, b) for lev in range(2) for a in range(CROWS) for b in range(CCOLS)]
    merge = []
    for da in range(2):
        for db in range(2):
            for group in range(2):
                merge += [place[(2 * group + lev, 2 * a + da, 2 * b + db)] for lev, a, b in coarse_cells]
                merge += [-1] * (SLAB - len(coarse_cells))
    merge = one_hot(merge, CELLS)
    compact = one_hot([group * SLAB + i for group in range(2) for i in range(36)], 2 * SLAB)
    band = one_hot(
        [d * 72 + k * 6 + c for k in range(12) for d in range(4) for c in range(6)], CELLS
    )
    return gather, scatter, to_window, from_window, merge, compact, band


def dot(a, b):
    return jnp.dot(a, b, preferred_element_type=F32)


def dot_t(a, b):
    return lax.dot_general(a, b, (((1,), (1,)), ((), ())), preferred_element_type=F32)


def norm_rows(values):
    mean = jnp.mean(values, -1, keepdims=True)
    centred = values - mean
    spread = jnp.mean(centred * centred, -1, keepdims=True)
    return centred * lax.rsqrt(spread + 1e-05)


def gelu(v):
    return 0.5 * v * (1.0 + lax.erf(v * np.float32(2.0**-0.5)))


def stack_slabs(ref, m):
    return jnp.concatenate([ref[m, q].astype(F32) for q in range(4)], axis=0).astype(BF16)


def attend(q_ref, q_rows, k_rows, q_at, k_at, v_at, bias):
    rows = q_rows[1]
    qp = q_ref[pl.ds(*q_rows), q_at : q_at + 128]
    kp = q_ref[pl.ds(*k_rows), k_at : k_at + 128]
    vp = q_ref[pl.ds(*k_rows), v_at : v_at + 128]
    first = lax.broadcasted_iota(jnp.int32, (rows, 128), 1) < 64
    outs = []
    for head in range(2):
        keep = first if head == 0 else ~first
        qh = jnp.where(keep, qp, jnp.zeros_like(qp))
        scores = dot_t(qh, kp) * 0.125 + bias
        weights = jnp.exp(scores - jnp.max(scores, -1, keepdims=True))
        total = jnp.sum(weights, -1, keepdims=True)
        outs.append(dot(weights.astype(BF16), vp) / total)
    return jnp.where(first, outs[0], outs[1])


def body(
    tok, gain1, gain2, gain_m, gain3, gather, scatter, to_win, from_win, merge, compact, band,
    qkv1_h, proj1_h, in_h, out_h, mw_h, qkv2_h, proj2_h,
    l1, l2,
    qkv1, proj1, w_in, w_out, mw, qkv2, proj2,
    xs, nrm, win, qkv, att, bko, bki, mid, acc, coarse, ns, nw, qkv_b, o2, at2, g,
    bias1, bias2,
    w_sem, hs, hr, bs, br, cs, cr, as_, ar, gs, gr,
):
    lat, lon = lax.axis_index("lat"), lax.axis_index("lon")
    north, south = lax.rem(lat + LAT - 1, LAT), lax.rem(lat + 1, LAT)
    west, east = lax.rem(lon + LON - 1, LON), lax.rem(lon + 1, LON)
    core = lax.rem(lon, 2)
    z = lax.rem(lon // 2, 4)
    yh = lon // 8
    lon_y = lax.rem(lon + 8, LON)
    zp, zm = lax.rem(z + 1, 4), lax.rem(z + 3, 4)
    z_far = lax.rem(z + 2, 4)
    other = lon + 1 - 2 * core

    def at(y, zz):
        return y * 8 + zz * 2 + core

    lon_zp, lon_zm = at(yh, zp), at(yh, zm)
    group_lat, group_lon = lat - lax.rem(lat, 2), lon - core
    level_group = lax.rem(lat, 2)
    mine = 2 * level_group + core
    peers = []
    for k in range(1, 4):
        j = lax.rem(mine + k, 4)
        peers.append((j, (group_lat + j // 2, group_lon + lax.rem(j, 2))))

    to_nbr = [(north, west), (north, lon), (lat, west)]
    from_nbr = [(south, east), (south, lon), (lat, east)]

    loads = []
    wide = HEADS2 // 2 * 64
    for i, (src, dst) in enumerate(
        [(qkv1_h, qkv1), (proj1_h, proj1), (in_h, w_in), (out_h, w_out), (mw_h, mw)]
    ):
        loads.append(pltpu.make_async_copy(src, dst, w_sem.at[i]))
    for part in range(3):
        columns = pl.ds(pl.multiple_of(part * D2 + core * wide, wide), wide)
        loads.append(
            pltpu.make_async_copy(
                qkv2_h.at[:, columns], qkv2.at[:, pl.ds(part * wide, wide)], w_sem.at[5 + part]
            )
        )
    loads.append(pltpu.make_async_copy(proj2_h, proj2, w_sem.at[8]))
    loads[0].start()

    barrier = pltpu.get_barrier_semaphore()
    partners = to_nbr + from_nbr + [dev for _, dev in peers]
    partners += [(lat, lon_y), (lat, lon_zp), (lat, lon_zm)]
    for dev in partners:
        pl.semaphore_signal(barrier, inc=1, device_id=dev, device_id_type=MESH)

    def remote(src, dst, send, recv, dev):
        return pltpu.make_async_remote_copy(
            src_ref=src, dst_ref=dst, send_sem=send, recv_sem=recv, device_id=dev, device_id_type=MESH
        )

    def halo(m, q):
        return remote(nrm.at[m, q], win.at[m, q], hs.at[m, q], hr.at[m, q], to_nbr[q])

    def back(m, q):
        return remote(bko.at[m, q], bki.at[m, q], bs.at[m, q], br.at[m, q], from_nbr[q])

    def spread(m, k):
        j, dev = peers[k]
        return remote(ns.at[m, j // 2], nw.at[m, mine], cs.at[m, k], cr.at[m, mine], dev)

    def spread_arrival(m, k):
        j, dev = peers[k]
        return remote(nw.at[m, j], nw.at[m, j], cs.at[m, k], cr.at[m, j], dev)

    def result(m, k):
        j, dev = peers[k]
        return remote(o2.at[m, j], at2.at[m, mine], as_.at[m, k], ar.at[m, mine], dev)

    def result_arrival(m, k):
        j, dev = peers[k]
        return remote(o2.at[m, j], at2.at[m, j], as_.at[m, k], ar.at[m, j], dev)

    def block(m, slot, send, dev):
        return remote(g.at[m, slot], g.at[m, slot], gs.at[m, send], gr.at[m, slot], (lat, dev))

    def arrived(m, slot):
        block(m, slot, 0, lon_y).wait_recv()

    def blocks_of(shape, dim, size):
        return lax.broadcasted_iota(jnp.int32, shape, dim) // size

    shape = (HALF, HALF)
    south_q = blocks_of(shape, 0, 72) != blocks_of(shape, 1, 72)
    level_a = lax.rem(blocks_of(shape, 0, 18), 2) != lax.rem(blocks_of(shape, 1, 18), 2)
    edge = jnp.where(lat == LAT - 1, np.float32(-1e30), np.float32(0.0))
    rows_bias = jnp.where(south_q, edge, 0.0)
    bias1[0] = rows_bias
    bias1[1] = jnp.where(level_a, np.float32(-1e30), rows_bias)
    empty = lax.rem(lax.broadcasted_iota(jnp.int32, (1, 4 * SLAB), 1), SLAB) >= 36
    bias2[...] = jnp.where(empty, np.float32(-1e30), np.float32(0.0))

    pl.semaphore_wait(barrier, len(partners))

    def start_member(m, carry):
        x = dot(gather[...], tok[m].astype(F32).reshape(CELLS, D).astype(BF16))
        xs[m] = x.astype(BF16)
        normed = (norm_rows(x) * gain1[...])
        for q in range(3):
            nrm[m, q] = normed[q * QUAD : (q + 1) * QUAD].astype(BF16)
            halo(m, q).start()
        win[m, 3] = normed[3 * QUAD :].astype(BF16)
        return carry

    lax.fori_loop(0, MEMBERS, start_member, 0)
    for load in loads[1:]:
        load.start()

    def window_attention(m):
        for q in range(3):
            halo(m, q).wait_recv()
        cells = dot(to_win[...], stack_slabs(win, m)).astype(BF16)
        for part in range(3):
            columns = slice(part * D, (part + 1) * D)
            qkv[:, columns] = dot(cells, qkv1[:, columns]).astype(BF16)
        for lp in range(2):
            rows = (lp * HALF, HALF)
            for pair in range(4):
                columns = pair * 128
                att[lp * HALF : (lp + 1) * HALF, columns : columns + 128] = attend(
                    qkv, rows, rows, columns, D + columns, 2 * D + columns, bias1[lp]
                ).astype(BF16)
        tile = dot(from_win[...], att[...])
        for q in range(3):
            bko[m, q] = tile[q * QUAD : (q + 1) * QUAD].astype(BF16)
            back(m, q).start()
        bki[m, 3] = tile[3 * QUAD :].astype(BF16)

    def feed_forward(m):
        for q in range(3):
            back(m, q).wait_recv()
        mid[...] = xs[m].astype(F32) + dot(stack_slabs(bki, m), proj1[...])
        normed = (norm_rows(mid[...]) * gain2[...]).astype(BF16)
        for part in range(4):
            columns = slice(part * D, (part + 1) * D)
            hidden = gelu(dot(normed, w_in[:, columns])).astype(BF16)
            partial = dot(hidden, w_out[columns, :])
            if part == 0:
                acc[...] = mid[...] + partial
            else:
                acc[...] += partial
        level1 = acc[...].astype(BF16)
        l1[m] = dot(scatter[...], level1).reshape(ROWS, COLS, LEVELS, D).astype(BF16)
        quarters = dot(merge[...], level1)
        parts = [quarters[k * 2 * SLAB : (k + 1) * 2 * SLAB] for k in range(4)]
        mean = sum(jnp.sum(p, -1, keepdims=True) for p in parts) * (1.0 / (4 * D))
        parts = [p - mean for p in parts]
        var = sum(jnp.sum(p * p, -1, keepdims=True) for p in parts) * (1.0 / (4 * D))
        scale = lax.rsqrt(var + 1e-05)
        merged = jnp.concatenate(
            [(p * scale * gain_m[:, k * D : (k + 1) * D]).astype(BF16) for k, p in enumerate(parts)],
            axis=1,
        )
        small = dot(merged, mw[...]).astype(BF16).astype(F32)
        coarse[m] = small
        normed3 = norm_rows(small) * gain3[...]
        for group in range(2):
            ns[m, group] = normed3[group * SLAB : (group + 1) * SLAB].astype(BF16)
        for k in range(3):
            spread(m, k).start()
        nw[m, mine] = ns[m, level_group]

    def heads_of_group(m):
        for k in range(3):
            spread_arrival(m, k).wait_recv()
        cells = stack_slabs(nw, m)
        for part in range(3):
            columns = slice(part * wide, (part + 1) * wide)
            qkv_b[:, columns] = dot(cells, qkv2[:, columns]).astype(BF16)
        rows = (0, 4 * SLAB)
        for pair in range(4):
            columns = pair * 128
            out = attend(qkv_b, rows, rows, columns, wide + columns, 2 * wide + columns, bias2[...])
            for d in range(4):
                o2[m, d, :, columns : columns + 128] = out[d * SLAB : (d + 1) * SLAB].astype(BF16)
        for k in range(3):
            result(m, k).start()
        at2[m, mine] = o2[m, mine]

    def project_out(m):
        for k in range(3):
            result_arrival(m, k).wait_recv()
        attended = jnp.concatenate(
            [
                jnp.concatenate([at2[m, 2 * group + half].astype(F32) for group in range(2)], axis=0)
                for half in range(2)
            ],
            axis=1,
        ).astype(BF16)
        level2 = (coarse[m] + dot(attended, proj2[...])).astype(BF16)
        g[m, lon] = dot(compact[...], level2).astype(BF16)
        block(m, lon, 0, lon_y).start()
        block(m, lon, 1, lon_zp).start()
        block(m, lon, 2, lon_zm).start()
        block(m, lon, 3, other).start()

    def after_y(m):
        arrived(m, lon_y)
        block(m, lon_y, 4, lon_zp).start()
        block(m, lon_y, 5, lon_zm).start()
        block(m, lon_y, 6, other).start()

    toward = 1 - 2 * core
    z_from = lax.rem(z + 4 - toward, 4)
    z_to = lax.rem(z + 4 + toward, 4)

    def after_z(m):
        for y in range(2):
            arrived(m, at(y, z_from))
            block(m, at(y, z_from), 7 + y, at(yh, z_to)).start()
            block(m, at(y, z_from), 9 + y, other).start()
        for y in range(2):
            arrived(m, at(y, z_to))
            block(m, at(y, z_to), 11 + y, other).start()

    def after_z2(m):
        for y in range(2):
            arrived(m, at(y, z_far))
            block(m, at(y, z_far), 13 + y, other).start()

    def lay_out(m):
        for y in range(2):
            for zz in range(4):
                arrived(m, y * 8 + zz * 2 + 1 - core)

        for half in range(2):
            pieces = []
            for quarter in range(2):
                first = half * 8 + quarter * 4
                slabs = jnp.concatenate([g[m, first + d].astype(F32) for d in range(4)], axis=0)
                pieces.append(dot(band[...], slabs.astype(BF16)).reshape(12, 24, D2))
            columns = jnp.concatenate(pieces, axis=1).astype(BF16)
            l2[m, :, :, half * 48 : (half + 1) * 48, :] = columns.reshape(LEVELS, CROWS, 48, D2)

    def when(t, lo, hi, phase, lag):
        @pl.when((t >= lo) & (t < hi))
        def _():
            phase(t - lag)

    def step(t, carry):
        @pl.when(t == 0)
        def _():
            loads[0].wait()

        when(t, 0, 4, window_attention, 0)

        @pl.when(t == 2)
        def _():
            for i in range(1, 5):
                loads[i].wait()

        when(t, 2, 6, feed_forward, 2)

        @pl.when(t == 3)
        def _():
            for i in range(5, 9):
                loads[i].wait()

        when(t, 4, 8, project_out, 4)
        when(t, 5, 9, after_z, 5)
        when(t, 3, 7, heads_of_group, 3)
        when(t, 4, 8, after_y, 4)
        when(t, 5, 9, after_z2, 5)
        when(t, 6, 10, lay_out, 6)
        return carry

    lax.fori_loop(0, 10, step, 0)

    def finish(m, carry):
        for q in range(3):
            halo(m, q).wait_send()
            back(m, q).wait_send()
            spread(m, q).wait_send()
            result(m, q).wait_send()
        for i in range(15):
            block(m, lon, i, lon_y).wait_send()
        return carry

    lax.fori_loop(0, MEMBERS, finish, 0)


def hand_out(l1_in, l2_in, l1, l2, sems):
    copies = [pltpu.make_async_copy(l2_in.at[m], l2.at[m], sems.at[m]) for m in range(MEMBERS)]
    copies.append(pltpu.make_async_copy(l1_in, l1, sems.at[MEMBERS]))
    for copy in copies:
        copy.start()
    for copy in copies:
        copy.wait()


def shards(
    tokens, norm1_gain, qkv1, proj1, norm2_gain, mlp_in, mlp_out, merge_gain, merge_weight,
    norm3_gain, qkv2, proj2,
):
    vmem = pl.BlockSpec(memory_space=pltpu.VMEM)
    hbm = pl.BlockSpec(memory_space=pl.ANY)
    dma = pltpu.SemaphoreType.DMA
    wide = HEADS2 // 2 * 64

    def bf(*dims):
        return pltpu.VMEM(dims, BF16)

    def fl(*dims):
        return pltpu.VMEM(dims, F32)

    level1, level2 = pl.pallas_call(
        body,
        name="encoder",
        out_shape=(
            pltpu.VMEM((MEMBERS, ROWS, COLS, LEVELS, D), BF16),
            pltpu.VMEM((MEMBERS, LEVELS, CROWS, LON * CCOLS, D2), BF16),
        ),
        in_specs=[vmem] * 12 + [hbm] * 7,
        out_specs=(vmem, vmem),
        scratch_shapes=[
            bf(D, 3 * D), bf(D, D), bf(D, 4 * D), bf(4 * D, D), bf(4 * D, D2), bf(D2, 3 * wide),
            bf(D2, D2),
            bf(MEMBERS, CELLS, D),
            bf(MEMBERS, 3, QUAD, D), bf(MEMBERS, 4, QUAD, D),
            bf(CELLS, 3 * D), bf(CELLS, D),
            bf(MEMBERS, 3, QUAD, D), bf(MEMBERS, 4, QUAD, D),
            fl(CELLS, D), fl(CELLS, D),
            fl(MEMBERS, 2 * SLAB, D2), bf(MEMBERS, 2, SLAB, D2), bf(MEMBERS, 4, SLAB, D2),
            bf(4 * SLAB, 3 * wide),
            bf(MEMBERS, 4, SLAB, wide), bf(MEMBERS, 4, SLAB, wide),
            bf(MEMBERS, LON, QUAD, D2),
            fl(2, HALF, HALF), fl(1, 4 * SLAB),
            dma((9,)),
            dma((MEMBERS, 3)), dma((MEMBERS, 3)),
            dma((MEMBERS, 3)), dma((MEMBERS, 3)),
            dma((MEMBERS, 3)), dma((MEMBERS, 4)),
            dma((MEMBERS, 3)), dma((MEMBERS, 4)),
            dma((MEMBERS, 15)), dma((MEMBERS, LON)),
        ],
        compiler_params=pltpu.CompilerParams(
            collective_id=0, has_side_effects=True, vmem_limit_bytes=48 * 2**20
        ),
        cost_estimate=pl.CostEstimate(flops=12 * 10**9, bytes_accessed=30 * 10**6, transcendentals=4 * 10**6),
    )(
        jnp.transpose(tokens, (0, 2, 3, 1, 4)), norm1_gain.reshape(1, D), norm2_gain.reshape(1, D), merge_gain.reshape(1, 4 * D),
        norm3_gain.reshape(1, D2), *[jnp.asarray(order) for order in reorderings()],
        qkv1, proj1, mlp_in, mlp_out, merge_weight, qkv2, proj2,
    )
    level1, level2 = pl.pallas_call(
        hand_out,
        name="hand_out",
        out_shape=(
            jax.ShapeDtypeStruct(level1.shape, BF16),
            jax.ShapeDtypeStruct(level2.shape, BF16),
        ),
        in_specs=[vmem, vmem],
        out_specs=(hbm, hbm),
        scratch_shapes=[dma((MEMBERS + 1,))],
        compiler_params=pltpu.CompilerParams(vmem_limit_bytes=2**20),
    )(level1, level2)
    return jnp.transpose(level1, (0, 3, 1, 2, 4)), level2


def solution(mesh):
    in_specs = (P(None, None, "lat", "lon", None),) + (P(),) * 11
    out_specs = (P(None, None, "lat", "lon", None), P(None, None, "lat", None, None))
    return jax.shard_map(shards, mesh=mesh, in_specs=in_specs, out_specs=out_specs, check_vma=False)
```

```python
import functools

import jax
import jax.numpy as jnp
import ml_dtypes
import numpy as np
from jax import lax
from jax.experimental import pallas as pl
from jax.experimental.pallas import tpu as pltpu
from jax.sharding import PartitionSpec as P

F32 = jnp.float32
BF16 = jnp.bfloat16
MESH = pl.DeviceIdType.MESH

MEMBERS, LEVELS, ROWS, COLS, D = 4, 4, 6, 12, 512
CELLS = LEVELS * ROWS * COLS
QUAD = CELLS // 4
SLAB = 40
LAT, LON = 8, 16
CROWS, CCOLS, D2 = 3, 6, 1024
HEADS2 = 16
HALF = 144


def quad_cells():
    cells = []
    for rh in range(2):
        for ch in range(2):
            for levels in ((1, 2), (0, 3)):
                for lev in levels:
                    for r in range(3):
                        for c in range(6):
                            cells.append((lev, rh * 3 + r, ch * 6 + c))
    return cells


def one_hot(rows, width):
    out = np.zeros((len(rows), width), ml_dtypes.bfloat16)
    for i, row in enumerate(rows):
        if row >= 0:
            out[i, row] = 1
    return out


def reorderings():
    cells = quad_cells()
    place = {cell: i for i, cell in enumerate(cells)}
    gather = one_hot([(r * COLS + c) * LEVELS + lev for lev, r, c in cells], CELLS)
    scatter = np.ascontiguousarray(gather.T)
    window_rows = [q * 72 + lp * 36 + i for lp in range(2) for q in range(4) for i in range(36)]
    to_window = one_hot(window_rows, CELLS)
    from_window = np.ascontiguousarray(to_window.T)
    coarse_cells = [(lev, a, b) for lev in range(2) for a in range(CROWS) for b in range(CCOLS)]
    merge = []
    for da in range(2):
        for db in range(2):
            for group in range(2):
                merge += [place[(2 * group + lev, 2 * a + da, 2 * b + db)] for lev, a, b in coarse_cells]
                merge += [-1] * (SLAB - len(coarse_cells))
    merge = one_hot(merge, CELLS)
    compact = one_hot([group * SLAB + i for group in range(2) for i in range(36)], 2 * SLAB)
    band = one_hot(
        [d * 72 + k * 6 + c for k in range(12) for d in range(4) for c in range(6)], CELLS
    )
    return gather, scatter, to_window, from_window, merge, compact, band


def dot(a, b):
    return jnp.dot(a, b, preferred_element_type=F32)


def dot_t(a, b):
    return lax.dot_general(a, b, (((1,), (1,)), ((), ())), preferred_element_type=F32)


def norm_rows(values):
    mean = jnp.mean(values, -1, keepdims=True)
    centred = values - mean
    spread = jnp.mean(centred * centred, -1, keepdims=True)
    return centred * lax.rsqrt(spread + 1e-05)


def gelu(v):
    return 0.5 * v * (1.0 + lax.erf(v * np.float32(2.0**-0.5)))


def stack_slabs(ref, m):
    return jnp.concatenate([ref[m, q].astype(F32) for q in range(4)], axis=0).astype(BF16)


def attend(q_ref, q_rows, k_rows, q_at, k_at, v_at, bias):
    rows = q_rows[1]
    qp = q_ref[pl.ds(*q_rows), q_at : q_at + 128]
    kp = q_ref[pl.ds(*k_rows), k_at : k_at + 128]
    vp = q_ref[pl.ds(*k_rows), v_at : v_at + 128]
    first = lax.broadcasted_iota(jnp.int32, (rows, 128), 1) < 64
    outs = []
    for head in range(2):
        keep = first if head == 0 else ~first
        qh = jnp.where(keep, qp, jnp.zeros_like(qp))
        scores = dot_t(qh, kp) * 0.125 + bias
        weights = jnp.exp(scores - jnp.max(scores, -1, keepdims=True))
        total = jnp.sum(weights, -1, keepdims=True)
        outs.append(dot(weights.astype(BF16), vp) / total)
    return jnp.where(first, outs[0], outs[1])


def body(
    tok, gain1, gain2, gain_m, gain3, gather, scatter, to_win, from_win, merge, compact, band,
    qkv1_h, proj1_h, in_h, out_h, mw_h, qkv2_h, proj2_h,
    l1, l2,
    qkv1, proj1, w_in, w_out, mw, qkv2, proj2,
    xs, nrm, win, qkv, att, bko, bki, mid, acc, coarse, ns, nw, qkv_b, o2, at2, g,
    bias1, bias2,
    w_sem, hs, hr, bs, br, cs, cr, as_, ar, gs, gr,
):
    lat, lon = lax.axis_index("lat"), lax.axis_index("lon")
    north, south = lax.rem(lat + LAT - 1, LAT), lax.rem(lat + 1, LAT)
    west, east = lax.rem(lon + LON - 1, LON), lax.rem(lon + 1, LON)
    core = lax.rem(lon, 2)
    z = lax.rem(lon // 2, 4)
    yh = lon // 8
    lon_y = lax.rem(lon + 8, LON)
    zp, zm = lax.rem(z + 1, 4), lax.rem(z + 3, 4)
    z_far = lax.rem(z + 2, 4)
    other = lon + 1 - 2 * core

    def at(y, zz):
        return y * 8 + zz * 2 + core

    lon_zp, lon_zm = at(yh, zp), at(yh, zm)
    group_lat, group_lon = lat - lax.rem(lat, 2), lon - core
    level_group = lax.rem(lat, 2)
    mine = 2 * level_group + core
    peers = []
    for k in range(1, 4):
        j = lax.rem(mine + k, 4)
        peers.append((j, (group_lat + j // 2, group_lon + lax.rem(j, 2))))

    to_nbr = [(north, west), (north, lon), (lat, west)]
    from_nbr = [(south, east), (south, lon), (lat, east)]

    def one_way(m, here, there):
        odd = lax.rem(m, 2)
        return tuple(a + odd * (b - a) for a, b in zip(here, there))

    def quadrant(m, k):
        return k + lax.rem(m, 2) * (3 - 2 * k)

    loads = []
    wide = HEADS2 // 2 * 64
    for i, (src, dst) in enumerate(
        [(qkv1_h, qkv1), (proj1_h, proj1), (in_h, w_in), (out_h, w_out), (mw_h, mw)]
    ):
        loads.append(pltpu.make_async_copy(src, dst, w_sem.at[i]))
    for part in range(3):
        columns = pl.ds(pl.multiple_of(part * D2 + core * wide, wide), wide)
        loads.append(
            pltpu.make_async_copy(
                qkv2_h.at[:, columns], qkv2.at[:, pl.ds(part * wide, wide)], w_sem.at[5 + part]
            )
        )
    loads.append(pltpu.make_async_copy(proj2_h, proj2, w_sem.at[8]))
    loads[0].start()

    barrier = pltpu.get_barrier_semaphore()
    partners = to_nbr + from_nbr + [dev for _, dev in peers]
    partners += [(lat, lon_y), (lat, lon_zp), (lat, lon_zm)]
    for dev in partners:
        pl.semaphore_signal(barrier, inc=1, device_id=dev, device_id_type=MESH)

    def remote(src, dst, send, recv, dev):
        return pltpu.make_async_remote_copy(
            src_ref=src, dst_ref=dst, send_sem=send, recv_sem=recv, device_id=dev, device_id_type=MESH
        )

    def halo(m, k):
        dev = one_way(m, to_nbr[k], from_nbr[k])
        q = quadrant(m, k)
        return remote(nrm.at[m, q], win.at[m, q], hs.at[m, k], hr.at[m, k], dev)

    def back(m, k):
        dev = one_way(m, from_nbr[k], to_nbr[k])
        q = quadrant(m, k)
        return remote(bko.at[m, q], bki.at[m, q], bs.at[m, k], br.at[m, k], dev)

    def spread(m, k):
        j, dev = peers[k]
        return remote(ns.at[m, j // 2], nw.at[m, mine], cs.at[m, k], cr.at[m, mine], dev)

    def spread_arrival(m, k):
        j, dev = peers[k]
        return remote(nw.at[m, j], nw.at[m, j], cs.at[m, k], cr.at[m, j], dev)

    def result(m, k):
        j, dev = peers[k]
        return remote(o2.at[m, j], at2.at[m, mine], as_.at[m, k], ar.at[m, mine], dev)

    def result_arrival(m, k):
        j, dev = peers[k]
        return remote(o2.at[m, j], at2.at[m, j], as_.at[m, k], ar.at[m, j], dev)

    def block(m, slot, send, dev):
        return remote(g.at[m, slot], g.at[m, slot], gs.at[m, send], gr.at[m, slot], (lat, dev))

    def arrived(m, slot):
        block(m, slot, 0, lon_y).wait_recv()

    def blocks_of(shape, dim, size):
        return lax.broadcasted_iota(jnp.int32, shape, dim) // size

    shape = (HALF, HALF)
    south_q = blocks_of(shape, 0, 72) != blocks_of(shape, 1, 72)
    level_a = lax.rem(blocks_of(shape, 0, 18), 2) != lax.rem(blocks_of(shape, 1, 18), 2)
    for odd, last in ((0, LAT - 1), (1, 0)):
        edge = jnp.where(lat == last, np.float32(-1e30), np.float32(0.0))
        rows_bias = jnp.where(south_q, edge, 0.0)
        bias1[odd, 0] = rows_bias
        bias1[odd, 1] = jnp.where(level_a, np.float32(-1e30), rows_bias)
    empty = lax.rem(lax.broadcasted_iota(jnp.int32, (1, 4 * SLAB), 1), SLAB) >= 36
    bias2[...] = jnp.where(empty, np.float32(-1e30), np.float32(0.0))

    def norm_member(m, carry):
        x = dot(gather[...], tok[m].astype(F32).reshape(CELLS, D).astype(BF16))
        xs[m] = x.astype(BF16)
        normed = (norm_rows(x) * gain1[...])
        for q in range(4):
            nrm[m, q] = normed[q * QUAD : (q + 1) * QUAD].astype(BF16)
        own = quadrant(m, 3)
        win[m, own] = nrm[m, own]
        return carry

    def send_halo(m):
        for k in range(3):
            halo(m, k).start()

    lax.fori_loop(0, 2, norm_member, 0)
    pl.semaphore_wait(barrier, len(partners))
    send_halo(0)
    send_halo(1)
    for load in loads[1:]:
        load.start()
    lax.fori_loop(2, MEMBERS, norm_member, 0)

    def window_attention(m):
        for k in range(3):
            halo(m, k).wait_recv()

        @pl.when(m < 2)
        def _():
            send_halo(m + 2)

        cells = dot(to_win[...], stack_slabs(win, m)).astype(BF16)
        for part in range(3):
            columns = slice(part * D, (part + 1) * D)
            qkv[:, columns] = dot(cells, qkv1[:, columns]).astype(BF16)
        for lp in range(2):
            rows = (lp * HALF, HALF)
            for pair in range(4):
                columns = pair * 128
                att[lp * HALF : (lp + 1) * HALF, columns : columns + 128] = attend(
                    qkv, rows, rows, columns, D + columns, 2 * D + columns, bias1[lax.rem(m, 2), lp]
                ).astype(BF16)
        tile = dot(from_win[...], att[...])
        for q in range(4):
            bko[m, q] = tile[q * QUAD : (q + 1) * QUAD].astype(BF16)
        for k in range(3):
            back(m, k).start()
        own = quadrant(m, 3)
        bki[m, own] = bko[m, own]

    def feed_forward(m):
        for k in range(3):
            back(m, k).wait_recv()
        mid[...] = xs[m].astype(F32) + dot(stack_slabs(bki, m), proj1[...])
        normed = (norm_rows(mid[...]) * gain2[...]).astype(BF16)
        for part in range(4):
            if part == 2:

                @pl.when(m == 3)
                def _():
                    after_y(0)

            columns = slice(part * D, (part + 1) * D)
            hidden = gelu(dot(normed, w_in[:, columns])).astype(BF16)
            partial = dot(hidden, w_out[columns, :])
            if part == 0:
                acc[...] = mid[...] + partial
            else:
                acc[...] += partial
        level1 = acc[...].astype(BF16)
        l1[m] = dot(scatter[...], level1).reshape(ROWS, COLS, LEVELS, D).astype(BF16)
        quarters = dot(merge[...], level1)
        parts = [quarters[k * 2 * SLAB : (k + 1) * 2 * SLAB] for k in range(4)]
        mean = sum(jnp.sum(p, -1, keepdims=True) for p in parts) * (1.0 / (4 * D))
        parts = [p - mean for p in parts]
        var = sum(jnp.sum(p * p, -1, keepdims=True) for p in parts) * (1.0 / (4 * D))
        scale = lax.rsqrt(var + 1e-05)
        merged = jnp.concatenate(
            [(p * scale * gain_m[:, k * D : (k + 1) * D]).astype(BF16) for k, p in enumerate(parts)],
            axis=1,
        )
        small = dot(merged, mw[...]).astype(BF16).astype(F32)
        coarse[m] = small
        normed3 = norm_rows(small) * gain3[...]
        for group in range(2):
            ns[m, group] = normed3[group * SLAB : (group + 1) * SLAB].astype(BF16)
        for k in range(3):
            spread(m, k).start()
        nw[m, mine] = ns[m, level_group]

    def heads_of_group(m):
        for k in range(3):
            spread_arrival(m, k).wait_recv()
        cells = stack_slabs(nw, m)
        for part in range(3):
            columns = slice(part * wide, (part + 1) * wide)
            qkv_b[:, columns] = dot(cells, qkv2[:, columns]).astype(BF16)
        rows = (0, 4 * SLAB)
        for pair in range(4):
            columns = pair * 128
            out = attend(qkv_b, rows, rows, columns, wide + columns, 2 * wide + columns, bias2[...])
            for d in range(4):
                o2[m, d, :, columns : columns + 128] = out[d * SLAB : (d + 1) * SLAB].astype(BF16)
        for k in range(3):
            result(m, k).start()
        at2[m, mine] = o2[m, mine]

    def project_out(m):
        for k in range(3):
            result_arrival(m, k).wait_recv()
        attended = jnp.concatenate(
            [
                jnp.concatenate([at2[m, 2 * group + half].astype(F32) for group in range(2)], axis=0)
                for half in range(2)
            ],
            axis=1,
        ).astype(BF16)
        level2 = (coarse[m] + dot(attended, proj2[...])).astype(BF16)
        g[m, lon] = dot(compact[...], level2).astype(BF16)
        block(m, lon, 0, lon_y).start()
        block(m, lon, 1, lon_zp).start()
        block(m, lon, 2, lon_zm).start()
        block(m, lon, 3, other).start()

    def after_y(m):
        arrived(m, lon_y)
        block(m, lon_y, 4, lon_zp).start()
        block(m, lon_y, 5, lon_zm).start()
        block(m, lon_y, 6, other).start()

    toward = 1 - 2 * core
    z_from = lax.rem(z + 4 - toward, 4)
    z_to = lax.rem(z + 4 + toward, 4)

    def after_z(m):
        for y in range(2):
            arrived(m, at(y, z_from))
            block(m, at(y, z_from), 7 + y, at(yh, z_to)).start()
            block(m, at(y, z_from), 9 + y, other).start()
        for y in range(2):
            arrived(m, at(y, z_to))
            block(m, at(y, z_to), 11 + y, other).start()

    def after_z2(m):
        for y in range(2):
            arrived(m, at(y, z_far))
            block(m, at(y, z_far), 13 + y, other).start()

    def lay_out(m):
        for y in range(2):
            for zz in range(4):
                arrived(m, y * 8 + zz * 2 + 1 - core)

        for half in range(2):
            pieces = []
            for quarter in range(2):
                first = half * 8 + quarter * 4
                slabs = jnp.concatenate([g[m, first + d].astype(F32) for d in range(4)], axis=0)
                pieces.append(dot(band[...], slabs.astype(BF16)).reshape(12, 24, D2))
            columns = jnp.concatenate(pieces, axis=1).astype(BF16)
            l2[m, :, :, half * 48 : (half + 1) * 48, :] = columns.reshape(LEVELS, CROWS, 48, D2)

    def when(t, lo, hi, phase, lag):
        @pl.when((t >= lo) & (t < hi))
        def _():
            phase(t - lag)

    def step(t, carry):
        @pl.when(t == 0)
        def _():
            loads[0].wait()

        when(t, 0, 4, window_attention, 0)

        @pl.when(t == 2)
        def _():
            for i in range(1, 5):
                loads[i].wait()

        when(t, 2, 6, feed_forward, 2)

        @pl.when(t == 3)
        def _():
            for i in range(5, 9):
                loads[i].wait()

        when(t, 4, 6, project_out, 4)
        when(t, 3, 6, heads_of_group, 3)
        return carry

    lax.fori_loop(0, 6, step, 0)
    heads_of_group(3)
    project_out(2)
    after_z(0)
    after_y(1)
    project_out(3)
    after_y(2)
    after_z(1)
    after_z2(0)
    after_y(3)
    after_z(2)
    after_z2(1)
    lay_out(0)
    after_z(3)
    after_z2(2)
    lay_out(1)
    after_z2(3)
    lay_out(2)
    lay_out(3)

    def finish(m, carry):
        for q in range(3):
            halo(m, q).wait_send()
            back(m, q).wait_send()
            spread(m, q).wait_send()
            result(m, q).wait_send()
        for i in range(15):
            block(m, lon, i, lon_y).wait_send()
        return carry

    lax.fori_loop(0, MEMBERS, finish, 0)


def hand_out(l1_in, l2_in, l1, l2, sems):
    copies = []
    for i in range(MEMBERS * LEVELS):
        m, lev = i // LEVELS, i % LEVELS
        copies.append(pltpu.make_async_copy(l2_in.at[m, lev], l2.at[m, lev], sems.at[i]))
    for m in range(MEMBERS):
        copies.append(pltpu.make_async_copy(l1_in.at[m], l1.at[m], sems.at[MEMBERS * LEVELS + m]))
    for copy in copies:
        copy.start()
    for copy in copies:
        copy.wait()


def shards(
    tokens, norm1_gain, qkv1, proj1, norm2_gain, mlp_in, mlp_out, merge_gain, merge_weight,
    norm3_gain, qkv2, proj2,
):
    vmem = pl.BlockSpec(memory_space=pltpu.VMEM)
    hbm = pl.BlockSpec(memory_space=pl.ANY)
    dma = pltpu.SemaphoreType.DMA
    wide = HEADS2 // 2 * 64

    def bf(*dims):
        return pltpu.VMEM(dims, BF16)

    def fl(*dims):
        return pltpu.VMEM(dims, F32)

    level1, level2 = pl.pallas_call(
        body,
        name="encoder",
        out_shape=(
            pltpu.VMEM((MEMBERS, ROWS, COLS, LEVELS, D), BF16),
            pltpu.VMEM((MEMBERS, LEVELS, CROWS, LON * CCOLS, D2), BF16),
        ),
        in_specs=[vmem] * 12 + [hbm] * 7,
        out_specs=(vmem, vmem),
        scratch_shapes=[
            bf(D, 3 * D), bf(D, D), bf(D, 4 * D), bf(4 * D, D), bf(4 * D, D2), bf(D2, 3 * wide),
            bf(D2, D2),
            bf(MEMBERS, CELLS, D),
            bf(MEMBERS, 4, QUAD, D), bf(MEMBERS, 4, QUAD, D),
            bf(CELLS, 3 * D), bf(CELLS, D),
            bf(MEMBERS, 4, QUAD, D), bf(MEMBERS, 4, QUAD, D),
            fl(CELLS, D), fl(CELLS, D),
            fl(MEMBERS, 2 * SLAB, D2), bf(MEMBERS, 2, SLAB, D2), bf(MEMBERS, 4, SLAB, D2),
            bf(4 * SLAB, 3 * wide),
            bf(MEMBERS, 4, SLAB, wide), bf(MEMBERS, 4, SLAB, wide),
            bf(MEMBERS, LON, QUAD, D2),
            fl(2, 2, HALF, HALF), fl(1, 4 * SLAB),
            dma((9,)),
            dma((MEMBERS, 3)), dma((MEMBERS, 3)),
            dma((MEMBERS, 3)), dma((MEMBERS, 3)),
            dma((MEMBERS, 3)), dma((MEMBERS, 4)),
            dma((MEMBERS, 3)), dma((MEMBERS, 4)),
            dma((MEMBERS, 15)), dma((MEMBERS, LON)),
        ],
        compiler_params=pltpu.CompilerParams(
            collective_id=0, has_side_effects=True, vmem_limit_bytes=48 * 2**20
        ),
        cost_estimate=pl.CostEstimate(flops=12 * 10**9, bytes_accessed=30 * 10**6, transcendentals=4 * 10**6),
    )(
        jnp.transpose(tokens, (0, 2, 3, 1, 4)), norm1_gain.reshape(1, D), norm2_gain.reshape(1, D), merge_gain.reshape(1, 4 * D),
        norm3_gain.reshape(1, D2), *[jnp.asarray(order) for order in reorderings()],
        qkv1, proj1, mlp_in, mlp_out, merge_weight, qkv2, proj2,
    )
    level1, level2 = pl.pallas_call(
        hand_out,
        name="hand_out",
        out_shape=(
            jax.ShapeDtypeStruct(level1.shape, BF16),
            jax.ShapeDtypeStruct(level2.shape, BF16),
        ),
        in_specs=[vmem, vmem],
        out_specs=(hbm, hbm),
        scratch_shapes=[dma((MEMBERS * (LEVELS + 1),))],
        compiler_params=pltpu.CompilerParams(vmem_limit_bytes=2**20),
    )(level1, level2)
    return jnp.transpose(level1, (0, 3, 1, 2, 4)), level2


def solution(mesh):
    in_specs = (P(None, None, "lat", "lon", None),) + (P(),) * 11
    out_specs = (P(None, None, "lat", "lon", None), P(None, None, "lat", None, None))
    return jax.shard_map(shards, mesh=mesh, in_specs=in_specs, out_specs=out_specs, check_vma=False)
```

```python
import functools

import jax
import jax.numpy as jnp
import ml_dtypes
import numpy as np
from jax import lax
from jax.experimental import pallas as pl
from jax.experimental.pallas import tpu as pltpu
from jax.sharding import PartitionSpec as P

F32 = jnp.float32
BF16 = jnp.bfloat16
MESH = pl.DeviceIdType.MESH

MEMBERS, LEVELS, ROWS, COLS, D = 4, 4, 6, 12, 512
CELLS = LEVELS * ROWS * COLS
QUAD = CELLS // 4
SLAB = 40
LAT, LON = 8, 16
CROWS, CCOLS, D2 = 3, 6, 1024
HEADS2 = 16
HALF = 144


def quad_cells():
    cells = []
    for rh in range(2):
        for ch in range(2):
            for levels in ((1, 2), (0, 3)):
                for lev in levels:
                    for r in range(3):
                        for c in range(6):
                            cells.append((lev, rh * 3 + r, ch * 6 + c))
    return cells


def one_hot(rows, width):
    out = np.zeros((len(rows), width), ml_dtypes.bfloat16)
    for i, row in enumerate(rows):
        if row >= 0:
            out[i, row] = 1
    return out


def reorderings():
    cells = quad_cells()
    place = {cell: i for i, cell in enumerate(cells)}
    gather = one_hot([(r * COLS + c) * LEVELS + lev for lev, r, c in cells], CELLS)
    scatter = np.ascontiguousarray(gather.T)
    window_rows = [q * 72 + lp * 36 + i for lp in range(2) for q in range(4) for i in range(36)]
    to_window = one_hot(window_rows, CELLS)
    from_window = np.ascontiguousarray(to_window.T)
    coarse_cells = [(lev, a, b) for lev in range(2) for a in range(CROWS) for b in range(CCOLS)]
    merge = []
    for da in range(2):
        for db in range(2):
            for group in range(2):
                merge += [place[(2 * group + lev, 2 * a + da, 2 * b + db)] for lev, a, b in coarse_cells]
                merge += [-1] * (SLAB - len(coarse_cells))
    merge = one_hot(merge, CELLS)
    compact = one_hot([group * SLAB + i for group in range(2) for i in range(36)], 2 * SLAB)
    band = one_hot(
        [d * 72 + k * 6 + c for k in range(12) for d in range(4) for c in range(6)], CELLS
    )
    return gather, scatter, to_window, from_window, merge, compact, band


def dot(a, b):
    return jnp.dot(a, b, preferred_element_type=F32)


def dot_t(a, b):
    return lax.dot_general(a, b, (((1,), (1,)), ((), ())), preferred_element_type=F32)


def norm_rows(values):
    mean = jnp.mean(values, -1, keepdims=True)
    centred = values - mean
    spread = jnp.mean(centred * centred, -1, keepdims=True)
    return centred * lax.rsqrt(spread + 1e-05)


def gelu(v):
    return 0.5 * v * (1.0 + lax.erf(v * np.float32(2.0**-0.5)))


def stack_slabs(ref, m):
    return jnp.concatenate([ref[m, q].astype(F32) for q in range(4)], axis=0).astype(BF16)


def attend(q_ref, q_rows, k_rows, q_at, k_at, v_at, bias):
    rows = q_rows[1]
    qp = q_ref[pl.ds(*q_rows), q_at : q_at + 128]
    kp = q_ref[pl.ds(*k_rows), k_at : k_at + 128]
    vp = q_ref[pl.ds(*k_rows), v_at : v_at + 128]
    first = lax.broadcasted_iota(jnp.int32, (rows, 128), 1) < 64
    outs = []
    for head in range(2):
        keep = first if head == 0 else ~first
        qh = jnp.where(keep, qp, jnp.zeros_like(qp))
        scores = dot_t(qh, kp) * 0.125 + bias
        weights = jnp.exp(scores - jnp.max(scores, -1, keepdims=True))
        total = jnp.sum(weights, -1, keepdims=True)
        outs.append(dot(weights.astype(BF16), vp) / total)
    return jnp.where(first, outs[0], outs[1])


def body(
    tok, gain1, gain2, gain_m, gain3, gather, scatter, to_win, from_win, merge, compact, band,
    qkv1_h, proj1_h, in_h, out_h, mw_h, qkv2_h, proj2_h,
    l1, l2,
    qkv1, proj1, w_in, w_out, mw, qkv2, proj2,
    xs, nrm, win, qkv, att, bko, bki, mid, acc, coarse, ns, nw, qkv_b, o2, at2, g,
    bias1, bias2,
    w_sem, hs, hr, bs, br, cs, cr, as_, ar, gs, gr,
):
    lat, lon = lax.axis_index("lat"), lax.axis_index("lon")
    north, south = lax.rem(lat + LAT - 1, LAT), lax.rem(lat + 1, LAT)
    west, east = lax.rem(lon + LON - 1, LON), lax.rem(lon + 1, LON)
    core = lax.rem(lon, 2)
    z = lax.rem(lon // 2, 4)
    yh = lon // 8
    lon_y = lax.rem(lon + 8, LON)
    zp, zm = lax.rem(z + 1, 4), lax.rem(z + 3, 4)
    z_far = lax.rem(z + 2, 4)
    other = lon + 1 - 2 * core

    def at(y, zz):
        return y * 8 + zz * 2 + core

    lon_zp, lon_zm = at(yh, zp), at(yh, zm)
    group_lat, group_lon = lat - lax.rem(lat, 2), lon - core
    level_group = lax.rem(lat, 2)
    mine = 2 * level_group + core
    peers = []
    for k in range(1, 4):
        j = lax.rem(mine + k, 4)
        peers.append((j, (group_lat + j // 2, group_lon + lax.rem(j, 2))))

    to_nbr = [(north, west), (north, lon), (lat, west)]
    from_nbr = [(south, east), (south, lon), (lat, east)]

    def one_way(m, here, there):
        odd = lax.rem(m, 2)
        return tuple(a + odd * (b - a) for a, b in zip(here, there))

    def quadrant(m, k):
        return k + lax.rem(m, 2) * (3 - 2 * k)

    loads = []
    wide = HEADS2 // 2 * 64
    for i, (src, dst) in enumerate(
        [(qkv1_h, qkv1), (proj1_h, proj1), (in_h, w_in), (out_h, w_out), (mw_h, mw)]
    ):
        loads.append(pltpu.make_async_copy(src, dst, w_sem.at[i]))
    for part in range(3):
        columns = pl.ds(pl.multiple_of(part * D2 + core * wide, wide), wide)
        loads.append(
            pltpu.make_async_copy(
                qkv2_h.at[:, columns], qkv2.at[:, pl.ds(part * wide, wide)], w_sem.at[5 + part]
            )
        )
    loads.append(pltpu.make_async_copy(proj2_h, proj2, w_sem.at[8]))
    loads[0].start()

    barrier = pltpu.get_barrier_semaphore()
    partners = to_nbr + from_nbr + [dev for _, dev in peers]
    partners += [(lat, lon_y), (lat, lon_zp), (lat, lon_zm)]
    for dev in partners:
        pl.semaphore_signal(barrier, inc=1, device_id=dev, device_id_type=MESH)

    def remote(src, dst, send, recv, dev):
        return pltpu.make_async_remote_copy(
            src_ref=src, dst_ref=dst, send_sem=send, recv_sem=recv, device_id=dev, device_id_type=MESH
        )

    def halo(m, k):
        dev = one_way(m, to_nbr[k], from_nbr[k])
        q = quadrant(m, k)
        return remote(nrm.at[m, q], win.at[m, q], hs.at[m, k], hr.at[m, k], dev)

    def back(m, k):
        dev = one_way(m, from_nbr[k], to_nbr[k])
        q = quadrant(m, k)
        return remote(bko.at[m, q], bki.at[m, q], bs.at[m, k], br.at[m, k], dev)

    across = 2 * (1 - level_group) + core
    diagonal = across + 1 - 2 * core
    beside = 2 * level_group + 1 - core
    to_across, to_beside = (group_lat + 1 - level_group, lon), (lat, other)

    def spread(m, k):
        src = (ns.at[m, 1 - level_group], ns.at[m, level_group], nw.at[m, across])[k]
        slot = (mine, mine, across)[k]
        dev = (to_across, to_beside, to_beside)[k]
        return remote(src, nw.at[m, slot], cs.at[m, k], cr.at[m, slot], dev)

    def spread_arrival(m, k):
        j = (across, beside, diagonal)[k]
        return remote(nw.at[m, j], nw.at[m, j], cs.at[m, k], cr.at[m, j], to_beside)

    def pass_on(m):
        spread_arrival(m, 0).wait_recv()
        spread(m, 2).start()

    def result(m, k):
        j, dev = peers[k]
        return remote(o2.at[m, j], at2.at[m, mine], as_.at[m, k], ar.at[m, mine], dev)

    def result_arrival(m, k):
        j, dev = peers[k]
        return remote(o2.at[m, j], at2.at[m, j], as_.at[m, k], ar.at[m, j], dev)

    def block(m, slot, send, dev):
        return remote(g.at[m, slot], g.at[m, slot], gs.at[m, send], gr.at[m, slot], (lat, dev))

    def arrived(m, slot):
        block(m, slot, 0, lon_y).wait_recv()

    def blocks_of(shape, dim, size):
        return lax.broadcasted_iota(jnp.int32, shape, dim) // size

    shape = (HALF, HALF)
    south_q = blocks_of(shape, 0, 72) != blocks_of(shape, 1, 72)
    level_a = lax.rem(blocks_of(shape, 0, 18), 2) != lax.rem(blocks_of(shape, 1, 18), 2)
    for odd, last in ((0, LAT - 1), (1, 0)):
        edge = jnp.where(lat == last, np.float32(-1e30), np.float32(0.0))
        rows_bias = jnp.where(south_q, edge, 0.0)
        bias1[odd, 0] = rows_bias
        bias1[odd, 1] = jnp.where(level_a, np.float32(-1e30), rows_bias)
    empty = lax.rem(lax.broadcasted_iota(jnp.int32, (1, 4 * SLAB), 1), SLAB) >= 36
    bias2[...] = jnp.where(empty, np.float32(-1e30), np.float32(0.0))

    def norm_member(m, carry):
        x = dot(gather[...], tok[m].astype(F32).reshape(CELLS, D).astype(BF16))
        xs[m] = x.astype(BF16)
        normed = (norm_rows(x) * gain1[...])
        for q in range(4):
            nrm[m, q] = normed[q * QUAD : (q + 1) * QUAD].astype(BF16)
        own = quadrant(m, 3)
        win[m, own] = nrm[m, own]
        return carry

    def send_halo(m):
        for k in range(3):
            halo(m, k).start()

    lax.fori_loop(0, 2, norm_member, 0)
    pl.semaphore_wait(barrier, len(partners))
    send_halo(0)
    send_halo(1)
    for load in loads[1:]:
        load.start()
    lax.fori_loop(2, MEMBERS, norm_member, 0)

    def window_attention(m):
        for k in range(3):
            halo(m, k).wait_recv()

        @pl.when(m < 2)
        def _():
            send_halo(m + 2)

        cells = dot(to_win[...], stack_slabs(win, m)).astype(BF16)
        for part in range(3):
            columns = slice(part * D, (part + 1) * D)
            qkv[:, columns] = dot(cells, qkv1[:, columns]).astype(BF16)
        for lp in range(2):
            rows = (lp * HALF, HALF)
            for pair in range(4):
                columns = pair * 128
                att[lp * HALF : (lp + 1) * HALF, columns : columns + 128] = attend(
                    qkv, rows, rows, columns, D + columns, 2 * D + columns, bias1[lax.rem(m, 2), lp]
                ).astype(BF16)
        tile = dot(from_win[...], att[...])
        for q in range(4):
            bko[m, q] = tile[q * QUAD : (q + 1) * QUAD].astype(BF16)
        for k in range(3):
            back(m, k).start()
        own = quadrant(m, 3)
        bki[m, own] = bko[m, own]

    def feed_forward(m):
        for k in range(3):
            back(m, k).wait_recv()
        mid[...] = xs[m].astype(F32) + dot(stack_slabs(bki, m), proj1[...])
        normed = (norm_rows(mid[...]) * gain2[...]).astype(BF16)
        for part in range(4):
            if part == 2:

                @pl.when(m >= 1)
                def _():
                    pass_on(m - 1)

            if part == 2:

                @pl.when(m == 3)
                def _():
                    after_y(0)

            columns = slice(part * D, (part + 1) * D)
            hidden = gelu(dot(normed, w_in[:, columns])).astype(BF16)
            partial = dot(hidden, w_out[columns, :])
            if part == 0:
                acc[...] = mid[...] + partial
            else:
                acc[...] += partial
        level1 = acc[...].astype(BF16)
        l1[m] = dot(scatter[...], level1).reshape(ROWS, COLS, LEVELS, D).astype(BF16)
        quarters = dot(merge[...], level1)
        parts = [quarters[k * 2 * SLAB : (k + 1) * 2 * SLAB] for k in range(4)]
        mean = sum(jnp.sum(p, -1, keepdims=True) for p in parts) * (1.0 / (4 * D))
        parts = [p - mean for p in parts]
        var = sum(jnp.sum(p * p, -1, keepdims=True) for p in parts) * (1.0 / (4 * D))
        scale = lax.rsqrt(var + 1e-05)
        merged = jnp.concatenate(
            [(p * scale * gain_m[:, k * D : (k + 1) * D]).astype(BF16) for k, p in enumerate(parts)],
            axis=1,
        )
        small = dot(merged, mw[...]).astype(BF16).astype(F32)
        coarse[m] = small
        normed3 = norm_rows(small) * gain3[...]
        for group in range(2):
            ns[m, group] = normed3[group * SLAB : (group + 1) * SLAB].astype(BF16)
        for k in range(2):
            spread(m, k).start()
        nw[m, mine] = ns[m, level_group]

    def heads_of_group(m):
        for k in range(1, 3):
            spread_arrival(m, k).wait_recv()
        cells = stack_slabs(nw, m)
        for part in range(3):
            columns = slice(part * wide, (part + 1) * wide)
            qkv_b[:, columns] = dot(cells, qkv2[:, columns]).astype(BF16)
        rows = (0, 4 * SLAB)
        for pair in range(4):
            columns = pair * 128
            out = attend(qkv_b, rows, rows, columns, wide + columns, 2 * wide + columns, bias2[...])
            for d in range(4):
                o2[m, d, :, columns : columns + 128] = out[d * SLAB : (d + 1) * SLAB].astype(BF16)
        for k in range(3):
            result(m, k).start()
        at2[m, mine] = o2[m, mine]

    def project_out(m):
        for k in range(3):
            result_arrival(m, k).wait_recv()
        attended = jnp.concatenate(
            [
                jnp.concatenate([at2[m, 2 * group + half].astype(F32) for group in range(2)], axis=0)
                for half in range(2)
            ],
            axis=1,
        ).astype(BF16)
        level2 = (coarse[m] + dot(attended, proj2[...])).astype(BF16)
        g[m, lon] = dot(compact[...], level2).astype(BF16)
        block(m, lon, 0, lon_y).start()
        block(m, lon, 1, lon_zp).start()
        block(m, lon, 2, lon_zm).start()
        block(m, lon, 3, other).start()

    def after_y(m):
        arrived(m, lon_y)
        block(m, lon_y, 4, lon_zp).start()
        block(m, lon_y, 5, lon_zm).start()
        block(m, lon_y, 6, other).start()

    toward = 1 - 2 * core
    z_from = lax.rem(z + 4 - toward, 4)
    z_to = lax.rem(z + 4 + toward, 4)

    def after_z(m):
        for y in range(2):
            arrived(m, at(y, z_from))
            block(m, at(y, z_from), 7 + y, at(yh, z_to)).start()
            block(m, at(y, z_from), 9 + y, other).start()
        for y in range(2):
            arrived(m, at(y, z_to))
            block(m, at(y, z_to), 11 + y, other).start()

    def after_z2(m):
        for y in range(2):
            arrived(m, at(y, z_far))
            block(m, at(y, z_far), 13 + y, other).start()

    def lay_out(m):
        for y in range(2):
            for zz in range(4):
                arrived(m, y * 8 + zz * 2 + 1 - core)

        for half in range(2):
            pieces = []
            for quarter in range(2):
                first = half * 8 + quarter * 4
                slabs = jnp.concatenate([g[m, first + d].astype(F32) for d in range(4)], axis=0)
                pieces.append(dot(band[...], slabs.astype(BF16)).reshape(12, 24, D2))
            columns = jnp.concatenate(pieces, axis=1).astype(BF16)
            l2[m, :, :, half * 48 : (half + 1) * 48, :] = columns.reshape(LEVELS, CROWS, 48, D2)

    def when(t, lo, hi, phase, lag):
        @pl.when((t >= lo) & (t < hi))
        def _():
            phase(t - lag)

    def step(t, carry):
        @pl.when(t == 0)
        def _():
            loads[0].wait()

        when(t, 0, 4, window_attention, 0)

        @pl.when(t == 2)
        def _():
            for i in range(1, 5):
                loads[i].wait()

        when(t, 2, 6, feed_forward, 2)

        @pl.when(t == 3)
        def _():
            for i in range(5, 9):
                loads[i].wait()

        when(t, 4, 6, project_out, 4)
        when(t, 3, 6, heads_of_group, 3)
        return carry

    lax.fori_loop(0, 6, step, 0)
    pass_on(3)
    after_z(0)
    project_out(2)
    heads_of_group(3)
    after_y(1)
    project_out(3)
    after_y(2)
    after_z(1)
    after_z2(0)
    after_y(3)
    after_z(2)
    after_z2(1)
    lay_out(0)
    after_z(3)
    after_z2(2)
    lay_out(1)
    after_z2(3)
    lay_out(2)
    lay_out(3)

    def finish(m, carry):
        for q in range(3):
            halo(m, q).wait_send()
            back(m, q).wait_send()
            spread(m, q).wait_send()
            result(m, q).wait_send()
        for i in range(15):
            block(m, lon, i, lon_y).wait_send()
        return carry

    lax.fori_loop(0, MEMBERS, finish, 0)


def hand_out(l1_in, l2_in, l1, l2, sems):
    copies = []
    for i in range(MEMBERS * LEVELS):
        m, lev = i // LEVELS, i % LEVELS
        copies.append(pltpu.make_async_copy(l2_in.at[m, lev], l2.at[m, lev], sems.at[i]))
    for m in range(MEMBERS):
        copies.append(pltpu.make_async_copy(l1_in.at[m], l1.at[m], sems.at[MEMBERS * LEVELS + m]))
    for copy in copies:
        copy.start()
    for copy in copies:
        copy.wait()


def shards(
    tokens, norm1_gain, qkv1, proj1, norm2_gain, mlp_in, mlp_out, merge_gain, merge_weight,
    norm3_gain, qkv2, proj2,
):
    vmem = pl.BlockSpec(memory_space=pltpu.VMEM)
    hbm = pl.BlockSpec(memory_space=pl.ANY)
    dma = pltpu.SemaphoreType.DMA
    wide = HEADS2 // 2 * 64

    def bf(*dims):
        return pltpu.VMEM(dims, BF16)

    def fl(*dims):
        return pltpu.VMEM(dims, F32)

    level1, level2 = pl.pallas_call(
        body,
        name="encoder",
        out_shape=(
            pltpu.VMEM((MEMBERS, ROWS, COLS, LEVELS, D), BF16),
            pltpu.VMEM((MEMBERS, LEVELS, CROWS, LON * CCOLS, D2), BF16),
        ),
        in_specs=[vmem] * 12 + [hbm] * 7,
        out_specs=(vmem, vmem),
        scratch_shapes=[
            bf(D, 3 * D), bf(D, D), bf(D, 4 * D), bf(4 * D, D), bf(4 * D, D2), bf(D2, 3 * wide),
            bf(D2, D2),
            bf(MEMBERS, CELLS, D),
            bf(MEMBERS, 4, QUAD, D), bf(MEMBERS, 4, QUAD, D),
            bf(CELLS, 3 * D), bf(CELLS, D),
            bf(MEMBERS, 4, QUAD, D), bf(MEMBERS, 4, QUAD, D),
            fl(CELLS, D), fl(CELLS, D),
            fl(MEMBERS, 2 * SLAB, D2), bf(MEMBERS, 2, SLAB, D2), bf(MEMBERS, 4, SLAB, D2),
            bf(4 * SLAB, 3 * wide),
            bf(MEMBERS, 4, SLAB, wide), bf(MEMBERS, 4, SLAB, wide),
            bf(MEMBERS, LON, QUAD, D2),
            fl(2, 2, HALF, HALF), fl(1, 4 * SLAB),
            dma((9,)),
            dma((MEMBERS, 3)), dma((MEMBERS, 3)),
            dma((MEMBERS, 3)), dma((MEMBERS, 3)),
            dma((MEMBERS, 3)), dma((MEMBERS, 4)),
            dma((MEMBERS, 3)), dma((MEMBERS, 4)),
            dma((MEMBERS, 15)), dma((MEMBERS, LON)),
        ],
        compiler_params=pltpu.CompilerParams(
            collective_id=0, has_side_effects=True, vmem_limit_bytes=48 * 2**20
        ),
        cost_estimate=pl.CostEstimate(flops=12 * 10**9, bytes_accessed=30 * 10**6, transcendentals=4 * 10**6),
    )(
        jnp.transpose(tokens, (0, 2, 3, 1, 4)), norm1_gain.reshape(1, D), norm2_gain.reshape(1, D), merge_gain.reshape(1, 4 * D),
        norm3_gain.reshape(1, D2), *[jnp.asarray(order) for order in reorderings()],
        qkv1, proj1, mlp_in, mlp_out, merge_weight, qkv2, proj2,
    )
    level1, level2 = pl.pallas_call(
        hand_out,
        name="hand_out",
        out_shape=(
            jax.ShapeDtypeStruct(level1.shape, BF16),
            jax.ShapeDtypeStruct(level2.shape, BF16),
        ),
        in_specs=[vmem, vmem],
        out_specs=(hbm, hbm),
        scratch_shapes=[dma((MEMBERS * (LEVELS + 1),))],
        compiler_params=pltpu.CompilerParams(vmem_limit_bytes=2**20),
    )(level1, level2)
    return jnp.transpose(level1, (0, 3, 1, 2, 4)), level2


def solution(mesh):
    in_specs = (P(None, None, "lat", "lon", None),) + (P(),) * 11
    out_specs = (P(None, None, "lat", "lon", None), P(None, None, "lat", None, None))
    return jax.shard_map(shards, mesh=mesh, in_specs=in_specs, out_specs=out_specs, check_vma=False)
```

```python
import functools

import jax
import jax.numpy as jnp
import ml_dtypes
import numpy as np
from jax import lax
from jax.experimental import pallas as pl
from jax.experimental.pallas import tpu as pltpu
from jax.sharding import PartitionSpec as P

F32 = jnp.float32
BF16 = jnp.bfloat16
MESH = pl.DeviceIdType.MESH

MEMBERS, LEVELS, ROWS, COLS, D = 4, 4, 6, 12, 512
CELLS = LEVELS * ROWS * COLS
QUAD = CELLS // 4
SLAB = 40
LAT, LON = 8, 16
CROWS, CCOLS, D2 = 3, 6, 1024
HEADS2 = 16
HALF = 144


def quad_cells():
    cells = []
    for rh in range(2):
        for ch in range(2):
            for levels in ((1, 2), (0, 3)):
                for lev in levels:
                    for r in range(3):
                        for c in range(6):
                            cells.append((lev, rh * 3 + r, ch * 6 + c))
    return cells


def one_hot(rows, width):
    out = np.zeros((len(rows), width), ml_dtypes.bfloat16)
    for i, row in enumerate(rows):
        if row >= 0:
            out[i, row] = 1
    return out


def reorderings():
    cells = quad_cells()
    place = {cell: i for i, cell in enumerate(cells)}
    gather = one_hot([(r * COLS + c) * LEVELS + lev for lev, r, c in cells], CELLS)
    scatter = np.ascontiguousarray(gather.T)
    window_rows = [q * 72 + lp * 36 + i for lp in range(2) for q in range(4) for i in range(36)]
    to_window = one_hot(window_rows, CELLS)
    from_window = np.ascontiguousarray(to_window.T)
    coarse_cells = [(lev, a, b) for lev in range(2) for a in range(CROWS) for b in range(CCOLS)]
    merge = []
    for da in range(2):
        for db in range(2):
            for group in range(2):
                merge += [place[(2 * group + lev, 2 * a + da, 2 * b + db)] for lev, a, b in coarse_cells]
                merge += [-1] * (SLAB - len(coarse_cells))
    merge = one_hot(merge, CELLS)
    compact = one_hot([group * SLAB + i for group in range(2) for i in range(36)], 2 * SLAB)
    band = one_hot(
        [d * 72 + k * 6 + c for k in range(12) for d in range(4) for c in range(6)], CELLS
    )
    return gather, scatter, to_window, from_window, merge, compact, band


def dot(a, b):
    return jnp.dot(a, b, preferred_element_type=F32)


def dot_t(a, b):
    return lax.dot_general(a, b, (((1,), (1,)), ((), ())), preferred_element_type=F32)


def norm_rows(values):
    mean = jnp.mean(values, -1, keepdims=True)
    centred = values - mean
    spread = jnp.mean(centred * centred, -1, keepdims=True)
    return centred * lax.rsqrt(spread + 1e-05)


def gelu(v):
    return 0.5 * v * (1.0 + lax.erf(v * np.float32(2.0**-0.5)))


def stack_slabs(ref, m):
    return jnp.concatenate([ref[m, q].astype(F32) for q in range(4)], axis=0).astype(BF16)


def attend(q_ref, q_rows, k_rows, q_at, k_at, v_at, bias):
    rows = q_rows[1]
    qp = q_ref[pl.ds(*q_rows), q_at : q_at + 128]
    kp = q_ref[pl.ds(*k_rows), k_at : k_at + 128]
    vp = q_ref[pl.ds(*k_rows), v_at : v_at + 128]
    first = lax.broadcasted_iota(jnp.int32, (rows, 128), 1) < 64
    outs = []
    for head in range(2):
        keep = first if head == 0 else ~first
        qh = jnp.where(keep, qp, jnp.zeros_like(qp))
        scores = dot_t(qh, kp) * 0.125 + bias
        weights = jnp.exp(scores - jnp.max(scores, -1, keepdims=True))
        total = jnp.sum(weights, -1, keepdims=True)
        outs.append(dot(weights.astype(BF16), vp) / total)
    return jnp.where(first, outs[0], outs[1])


def body(
    tok, gain1, gain2, gain_m, gain3, gather, scatter, to_win, from_win, merge, compact, band,
    qkv1_h, proj1_h, in_h, out_h, mw_h, qkv2_h, proj2_h,
    l1, l2,
    qkv1, proj1, w_in, w_out, mw, qkv2, proj2,
    xs, nrm, win, qkv, att, bko, bki, mid, acc, coarse, ns, nw, qkv_b, o2, at2, g,
    bias1, bias2,
    w_sem, hs, hr, bs, br, cs, cr, as_, ar, gs, gr,
):
    lat, lon = lax.axis_index("lat"), lax.axis_index("lon")
    north, south = lax.rem(lat + LAT - 1, LAT), lax.rem(lat + 1, LAT)
    west, east = lax.rem(lon + LON - 1, LON), lax.rem(lon + 1, LON)
    core = lax.rem(lon, 2)
    z = lax.rem(lon // 2, 4)
    yh = lon // 8
    lon_y = lax.rem(lon + 8, LON)
    zp, zm = lax.rem(z + 1, 4), lax.rem(z + 3, 4)
    z_far = lax.rem(z + 2, 4)
    other = lon + 1 - 2 * core

    def at(y, zz):
        return y * 8 + zz * 2 + core

    lon_zp, lon_zm = at(yh, zp), at(yh, zm)
    group_lat, group_lon = lat - lax.rem(lat, 2), lon - core
    level_group = lax.rem(lat, 2)
    mine = 2 * level_group + core
    peers = []
    for k in range(1, 4):
        j = lax.rem(mine + k, 4)
        peers.append((j, (group_lat + j // 2, group_lon + lax.rem(j, 2))))

    to_nbr = [(north, west), (north, lon), (lat, west)]
    from_nbr = [(south, east), (south, lon), (lat, east)]

    def one_way(m, here, there):
        odd = lax.rem(m, 2)
        return tuple(a + odd * (b - a) for a, b in zip(here, there))

    def quadrant(m, k):
        return k + lax.rem(m, 2) * (3 - 2 * k)

    loads = []
    wide = HEADS2 // 2 * 64
    for i, (src, dst) in enumerate(
        [(qkv1_h, qkv1), (proj1_h, proj1), (in_h, w_in), (out_h, w_out), (mw_h, mw)]
    ):
        loads.append(pltpu.make_async_copy(src, dst, w_sem.at[i]))
    for part in range(3):
        columns = pl.ds(pl.multiple_of(part * D2 + core * wide, wide), wide)
        loads.append(
            pltpu.make_async_copy(
                qkv2_h.at[:, columns], qkv2.at[:, pl.ds(part * wide, wide)], w_sem.at[5 + part]
            )
        )
    loads.append(pltpu.make_async_copy(proj2_h, proj2, w_sem.at[8]))
    loads[0].start()

    barrier = pltpu.get_barrier_semaphore()
    partners = to_nbr + from_nbr + [dev for _, dev in peers]
    partners += [(lat, lon_y), (lat, lon_zp), (lat, lon_zm)]
    for dev in partners:
        pl.semaphore_signal(barrier, inc=1, device_id=dev, device_id_type=MESH)

    def remote(src, dst, send, recv, dev):
        return pltpu.make_async_remote_copy(
            src_ref=src, dst_ref=dst, send_sem=send, recv_sem=recv, device_id=dev, device_id_type=MESH
        )

    def halo(m, k):
        dev = one_way(m, to_nbr[k], from_nbr[k])
        q = quadrant(m, k)
        return remote(nrm.at[m, q], win.at[m, q], hs.at[m, k], hr.at[m, k], dev)

    def back(m, k):
        dev = one_way(m, from_nbr[k], to_nbr[k])
        q = quadrant(m, k)
        return remote(bko.at[m, q], bki.at[m, q], bs.at[m, k], br.at[m, k], dev)

    across = 2 * (1 - level_group) + core
    diagonal = across + 1 - 2 * core
    beside = 2 * level_group + 1 - core
    to_across, to_beside = (group_lat + 1 - level_group, lon), (lat, other)

    def spread(m, k):
        src = (ns.at[m, 1 - level_group], ns.at[m, level_group], nw.at[m, across])[k]
        slot = (mine, mine, across)[k]
        dev = (to_across, to_beside, to_beside)[k]
        return remote(src, nw.at[m, slot], cs.at[m, k], cr.at[m, slot], dev)

    def spread_arrival(m, k):
        j = (across, beside, diagonal)[k]
        return remote(nw.at[m, j], nw.at[m, j], cs.at[m, k], cr.at[m, j], to_beside)

    def pass_on(m):
        spread_arrival(m, 0).wait_recv()
        spread(m, 2).start()

    def result(m, k):
        j, dev = peers[k]
        return remote(o2.at[m, j], at2.at[m, mine], as_.at[m, k], ar.at[m, mine], dev)

    def result_arrival(m, k):
        j, dev = peers[k]
        return remote(o2.at[m, j], at2.at[m, j], as_.at[m, k], ar.at[m, j], dev)

    def block(m, slot, send, dev):
        return remote(g.at[m, slot], g.at[m, slot], gs.at[m, send], gr.at[m, slot], (lat, dev))

    def arrived(m, slot):
        block(m, slot, 0, lon_y).wait_recv()

    def blocks_of(shape, dim, size):
        return lax.broadcasted_iota(jnp.int32, shape, dim) // size

    shape = (HALF, HALF)
    south_q = blocks_of(shape, 0, 72) != blocks_of(shape, 1, 72)
    level_a = lax.rem(blocks_of(shape, 0, 18), 2) != lax.rem(blocks_of(shape, 1, 18), 2)
    for odd, last in ((0, LAT - 1), (1, 0)):
        edge = jnp.where(lat == last, np.float32(-1e30), np.float32(0.0))
        rows_bias = jnp.where(south_q, edge, 0.0)
        bias1[odd, 0] = rows_bias
        bias1[odd, 1] = jnp.where(level_a, np.float32(-1e30), rows_bias)
    empty = lax.rem(lax.broadcasted_iota(jnp.int32, (1, 4 * SLAB), 1), SLAB) >= 36
    bias2[...] = jnp.where(empty, np.float32(-1e30), np.float32(0.0))

    def norm_member(m, carry):
        x = dot(gather[...], tok[m].astype(F32).reshape(CELLS, D).astype(BF16))
        xs[m] = x.astype(BF16)
        normed = (norm_rows(x) * gain1[...])
        for q in range(4):
            nrm[m, q] = normed[q * QUAD : (q + 1) * QUAD].astype(BF16)
        own = quadrant(m, 3)
        win[m, own] = nrm[m, own]
        return carry

    def send_halo(m):
        for k in range(3):
            halo(m, k).start()

    lax.fori_loop(0, 2, norm_member, 0)
    pl.semaphore_wait(barrier, len(partners))
    send_halo(0)
    send_halo(1)
    for load in loads[1:]:
        load.start()
    lax.fori_loop(2, MEMBERS, norm_member, 0)

    def window_attention(m):
        for k in range(3):
            halo(m, k).wait_recv()

        @pl.when(m < 2)
        def _():
            send_halo(m + 2)

        cells = dot(to_win[...], stack_slabs(win, m)).astype(BF16)
        for part in range(3):
            columns = slice(part * D, (part + 1) * D)
            qkv[:, columns] = dot(cells, qkv1[:, columns]).astype(BF16)
        for lp in range(2):
            rows = (lp * HALF, HALF)
            for pair in range(4):
                columns = pair * 128
                att[lp * HALF : (lp + 1) * HALF, columns : columns + 128] = attend(
                    qkv, rows, rows, columns, D + columns, 2 * D + columns, bias1[lax.rem(m, 2), lp]
                ).astype(BF16)
        tile = dot(from_win[...], att[...])
        for q in range(4):
            bko[m, q] = tile[q * QUAD : (q + 1) * QUAD].astype(BF16)
        for k in range(3):
            back(m, k).start()
        own = quadrant(m, 3)
        bki[m, own] = bko[m, own]

    def feed_forward(m):
        for k in range(3):
            back(m, k).wait_recv()
        mid[...] = xs[m].astype(F32) + dot(stack_slabs(bki, m), proj1[...])
        normed = (norm_rows(mid[...]) * gain2[...]).astype(BF16)
        for part in range(4):
            if part == 2:

                @pl.when(m >= 1)
                def _():
                    pass_on(m - 1)

            if part == 2:

                @pl.when(m == 3)
                def _():
                    after_y(0)

            columns = slice(part * D, (part + 1) * D)
            hidden = gelu(dot(normed, w_in[:, columns])).astype(BF16)
            partial = dot(hidden, w_out[columns, :])
            if part == 0:
                acc[...] = mid[...] + partial
            else:
                acc[...] += partial
        level1 = acc[...].astype(BF16)
        l1[m] = dot(scatter[...], level1).reshape(ROWS, COLS, LEVELS, D).astype(BF16)
        quarters = dot(merge[...], level1)
        parts = [quarters[k * 2 * SLAB : (k + 1) * 2 * SLAB] for k in range(4)]
        mean = sum(jnp.sum(p, -1, keepdims=True) for p in parts) * (1.0 / (4 * D))
        parts = [p - mean for p in parts]
        var = sum(jnp.sum(p * p, -1, keepdims=True) for p in parts) * (1.0 / (4 * D))
        scale = lax.rsqrt(var + 1e-05)
        merged = jnp.concatenate(
            [(p * scale * gain_m[:, k * D : (k + 1) * D]).astype(BF16) for k, p in enumerate(parts)],
            axis=1,
        )
        small = dot(merged, mw[...]).astype(BF16).astype(F32)
        coarse[m] = small
        normed3 = norm_rows(small) * gain3[...]
        for group in range(2):
            ns[m, group] = normed3[group * SLAB : (group + 1) * SLAB].astype(BF16)
        for k in range(2):
            spread(m, k).start()
        nw[m, mine] = ns[m, level_group]

    def heads_of_group(m):
        for k in range(1, 3):
            spread_arrival(m, k).wait_recv()
        cells = stack_slabs(nw, m)
        for part in range(3):
            columns = slice(part * wide, (part + 1) * wide)
            qkv_b[:, columns] = dot(cells, qkv2[:, columns]).astype(BF16)
        rows = (0, 4 * SLAB)
        for pair in range(4):
            columns = pair * 128
            out = attend(qkv_b, rows, rows, columns, wide + columns, 2 * wide + columns, bias2[...])
            for d in range(4):
                o2[m, d, :, columns : columns + 128] = out[d * SLAB : (d + 1) * SLAB].astype(BF16)
        for k in range(3):
            result(m, k).start()
        at2[m, mine] = o2[m, mine]

    def project_out(m):
        for k in range(3):
            result_arrival(m, k).wait_recv()
        attended = jnp.concatenate(
            [
                jnp.concatenate([at2[m, 2 * group + half].astype(F32) for group in range(2)], axis=0)
                for half in range(2)
            ],
            axis=1,
        ).astype(BF16)
        level2 = (coarse[m] + dot(attended, proj2[...])).astype(BF16)
        g[m, lon] = dot(compact[...], level2).astype(BF16)
        block(m, lon, 0, lon_y).start()
        block(m, lon, 1, lon_zp).start()
        block(m, lon, 2, lon_zm).start()
        block(m, lon, 3, other).start()

    def after_y(m):
        arrived(m, lon_y)
        block(m, lon_y, 4, lon_zp).start()
        block(m, lon_y, 5, lon_zm).start()
        block(m, lon_y, 6, other).start()

    toward = 1 - 2 * core
    z_from = lax.rem(z + 4 - toward, 4)
    z_to = lax.rem(z + 4 + toward, 4)

    def after_z(m):
        for y in range(2):
            arrived(m, at(y, z_from))
            block(m, at(y, z_from), 7 + y, at(yh, z_to)).start()
            block(m, at(y, z_from), 9 + y, other).start()
        for y in range(2):
            arrived(m, at(y, z_to))
            block(m, at(y, z_to), 11 + y, other).start()

    def after_z2(m):
        for y in range(2):
            arrived(m, at(y, z_far))
            block(m, at(y, z_far), 13 + y, other).start()

    def lay_out(m):
        for y in range(2):
            for zz in range(4):
                arrived(m, y * 8 + zz * 2 + 1 - core)

        for half in range(2):
            pieces = []
            for quarter in range(2):
                first = half * 8 + quarter * 4
                slabs = jnp.concatenate([g[m, first + d].astype(F32) for d in range(4)], axis=0)
                pieces.append(dot(band[...], slabs.astype(BF16)).reshape(12, 24, D2))
            columns = jnp.concatenate(pieces, axis=1).astype(BF16)
            l2[m, :, :, half * 48 : (half + 1) * 48, :] = columns.reshape(LEVELS, CROWS, 48, D2)

    def when(t, lo, hi, phase, lag):
        @pl.when((t >= lo) & (t < hi))
        def _():
            phase(t - lag)

    def step(t, carry):
        @pl.when(t == 0)
        def _():
            loads[0].wait()

        when(t, 0, 4, window_attention, 0)

        @pl.when(t == 2)
        def _():
            for i in range(1, 5):
                loads[i].wait()

        when(t, 2, 6, feed_forward, 2)

        @pl.when(t == 3)
        def _():
            for i in range(5, 9):
                loads[i].wait()

        when(t, 4, 6, project_out, 4)
        when(t, 3, 6, heads_of_group, 3)
        return carry

    lax.fori_loop(0, 6, step, 0)
    pass_on(3)
    after_z(0)
    project_out(2)
    after_y(1)
    heads_of_group(3)
    project_out(3)
    after_y(2)
    after_z(1)
    after_z2(0)
    after_y(3)
    after_z(2)
    after_z2(1)
    lay_out(0)
    after_z(3)
    after_z2(2)
    lay_out(1)
    after_z2(3)
    lay_out(2)
    lay_out(3)

    def finish(m, carry):
        for q in range(3):
            halo(m, q).wait_send()
            back(m, q).wait_send()
            spread(m, q).wait_send()
            result(m, q).wait_send()
        for i in range(15):
            block(m, lon, i, lon_y).wait_send()
        return carry

    lax.fori_loop(0, MEMBERS, finish, 0)


def hand_out(l1_in, l2_in, l1, l2, sems):
    copies = []
    for i in range(MEMBERS * LEVELS):
        m, lev = i // LEVELS, i % LEVELS
        copies.append(pltpu.make_async_copy(l2_in.at[m, lev], l2.at[m, lev], sems.at[i]))
    for m in range(MEMBERS):
        copies.append(pltpu.make_async_copy(l1_in.at[m], l1.at[m], sems.at[MEMBERS * LEVELS + m]))
    for copy in copies:
        copy.start()
    for copy in copies:
        copy.wait()


def shards(
    tokens, norm1_gain, qkv1, proj1, norm2_gain, mlp_in, mlp_out, merge_gain, merge_weight,
    norm3_gain, qkv2, proj2,
):
    vmem = pl.BlockSpec(memory_space=pltpu.VMEM)
    hbm = pl.BlockSpec(memory_space=pl.ANY)
    dma = pltpu.SemaphoreType.DMA
    wide = HEADS2 // 2 * 64

    def bf(*dims):
        return pltpu.VMEM(dims, BF16)

    def fl(*dims):
        return pltpu.VMEM(dims, F32)

    level1, level2 = pl.pallas_call(
        body,
        name="encoder",
        out_shape=(
            pltpu.VMEM((MEMBERS, ROWS, COLS, LEVELS, D), BF16),
            pltpu.VMEM((MEMBERS, LEVELS, CROWS, LON * CCOLS, D2), BF16),
        ),
        in_specs=[vmem] * 12 + [hbm] * 7,
        out_specs=(vmem, vmem),
        scratch_shapes=[
            bf(D, 3 * D), bf(D, D), bf(D, 4 * D), bf(4 * D, D), bf(4 * D, D2), bf(D2, 3 * wide),
            bf(D2, D2),
            bf(MEMBERS, CELLS, D),
            bf(MEMBERS, 4, QUAD, D), bf(MEMBERS, 4, QUAD, D),
            bf(CELLS, 3 * D), bf(CELLS, D),
            bf(MEMBERS, 4, QUAD, D), bf(MEMBERS, 4, QUAD, D),
            fl(CELLS, D), fl(CELLS, D),
            fl(MEMBERS, 2 * SLAB, D2), bf(MEMBERS, 2, SLAB, D2), bf(MEMBERS, 4, SLAB, D2),
            bf(4 * SLAB, 3 * wide),
            bf(MEMBERS, 4, SLAB, wide), bf(MEMBERS, 4, SLAB, wide),
            bf(MEMBERS, LON, QUAD, D2),
            fl(2, 2, HALF, HALF), fl(1, 4 * SLAB),
            dma((9,)),
            dma((MEMBERS, 3)), dma((MEMBERS, 3)),
            dma((MEMBERS, 3)), dma((MEMBERS, 3)),
            dma((MEMBERS, 3)), dma((MEMBERS, 4)),
            dma((MEMBERS, 3)), dma((MEMBERS, 4)),
            dma((MEMBERS, 15)), dma((MEMBERS, LON)),
        ],
        compiler_params=pltpu.CompilerParams(
            collective_id=0, has_side_effects=True, vmem_limit_bytes=48 * 2**20
        ),
        cost_estimate=pl.CostEstimate(flops=12 * 10**9, bytes_accessed=30 * 10**6, transcendentals=4 * 10**6),
    )(
        jnp.transpose(tokens, (0, 2, 3, 1, 4)), norm1_gain.reshape(1, D), norm2_gain.reshape(1, D), merge_gain.reshape(1, 4 * D),
        norm3_gain.reshape(1, D2), *[jnp.asarray(order) for order in reorderings()],
        qkv1, proj1, mlp_in, mlp_out, merge_weight, qkv2, proj2,
    )
    level1, level2 = pl.pallas_call(
        hand_out,
        name="hand_out",
        out_shape=(
            jax.ShapeDtypeStruct(level1.shape, BF16),
            jax.ShapeDtypeStruct(level2.shape, BF16),
        ),
        in_specs=[vmem, vmem],
        out_specs=(hbm, hbm),
        scratch_shapes=[dma((MEMBERS * (LEVELS + 1),))],
        compiler_params=pltpu.CompilerParams(vmem_limit_bytes=2**20),
    )(level1, level2)
    return jnp.transpose(level1, (0, 3, 1, 2, 4)), level2


def solution(mesh):
    in_specs = (P(None, None, "lat", "lon", None),) + (P(),) * 11
    out_specs = (P(None, None, "lat", "lon", None), P(None, None, "lat", None, None))
    return jax.shard_map(shards, mesh=mesh, in_specs=in_specs, out_specs=out_specs, check_vma=False)
```
